128 devices in a mesh: row: 8 (over x, core), col: 16 (over y, z).
Axes of the slice: x: 4, y: 4, z: 4, core: 2. Of those that a mesh axis runs over, the one named last changes fastest.
Arguments:
- front_inverse: float32 [16384, 16384], P('row', 'col'), as said below
- panel_front: float32 [4, 16384, 256], P(None, 'row'), may hold values from -0.0625 to 0.0625
- panel_cross: float32 [4, 4, 256, 256], replicated, may hold values from -0.375 to 0.375
- diag_inverse: float32 [4, 256, 256], replicated, may hold values from -6 to 6
- pattern: int32 [4, 40], replicated, may hold values from 0 to 63, as said below
Outputs:
- front_columns: float32 [4, 16384, 256], P(None, ('row', 'col'))
- panel_inverse: float32 [4, 4, 256, 256], replicated
The draws below stay inside these ranges and needn't reach their ends.
Inputs may be any that keep to these rules, and one draw needn't show every extreme that they name: `pattern`: each row holds 40 different block numbers; block 0 and block 63 are in every row. `front_inverse`: symmetric.
All inputs are finite; a program needn't handle non-finite values.
Results may differ from the reference program's by a relative error of at most 0.0001.
Values sent between devices are 32-bit elements; how exact they have to be, the bound alone decides.
A program may use at most 128 MiB of HBM per device.

```python
import jax
import jax.numpy as jnp
from jax import lax

BLOCK = 256
NB = 64
NNZ = 40
PANELS = 4
ORDER = 16384


def draw_front_inverse(key, part):
    key = jax.random.fold_in(key, 11)
    base = jax.random.normal(key, (NB * BLOCK, NB * BLOCK), jnp.float32)
    return (base + base.T) * 0.70710678


def draw_pattern(key, part):
    key = jax.random.fold_in(key, 23)
    rows_list = []
    for panel in range(PANELS):
        order_keys = jax.random.permutation(jax.random.fold_in(key, panel), NB - 2) + 1
        chosen = order_keys[:NNZ - 2].astype(jnp.int32)
        rows_list.append(jnp.concatenate([chosen, jnp.array([0, NB - 1], jnp.int32)]))
    return jnp.stack(rows_list)


def block_scale(stream_key, shape, pieces, low, largest):
    loudness = 1.0
    for position, shards_of in pieces:
        steps = jax.random.uniform(jax.random.fold_in(jax.random.fold_in(stream_key, 6), position), (shards_of,), jnp.float32, low / len(pieces), largest / len(pieces))
        loudness = loudness * jnp.repeat(jnp.exp(steps), shape[position] // shards_of).reshape((-1,) + (1,) * (len(shape) - 1 - position))
    return loudness


def noise(key, extent, scale, most, shards=(), held_as=jnp.bfloat16):
    result = scale * jax.random.normal(key, extent, jnp.float32)
    if shards:
        result = result * block_scale(key, extent, shards, -0.22, 0.18)
    return jnp.clip(result, -most, most).astype(held_as)


def setup_inputs(seed: int = 0) -> dict:
    seeds = jax.random.split(jax.random.key(seed), 6)
    return {
        "front_inverse": draw_front_inverse(jax.random.fold_in(seeds[5], 71), 0),
        "panel_front": noise(seeds[1], (PANELS, ORDER, BLOCK), (NNZ * BLOCK) ** -0.5, 0.0625, ((1, 8),), jnp.float32),
        "panel_cross": noise(seeds[2], (PANELS, PANELS, BLOCK, BLOCK), BLOCK ** -0.5, 0.375, (), jnp.float32),
        "diag_inverse": noise(seeds[3], (PANELS, BLOCK, BLOCK), 1.0, 6.0, (), jnp.float32),
        "pattern": draw_pattern(jax.random.fold_in(seeds[5], 71), 0),
    }


def product(left, right):
    return jnp.dot(left, right, precision=lax.Precision.HIGHEST, preferred_element_type=jnp.float32)


def inner(left, right):
    return jnp.einsum("ri,rj->ij", left, right, precision=lax.Precision.HIGHEST, preferred_element_type=jnp.float32)


def reference(front_inverse, panel_front, panel_cross, diag_inverse, pattern):
    block_ids = jnp.arange(NB * BLOCK, dtype=jnp.int32) // BLOCK
    member = jnp.any(block_ids[None, :, None] == pattern[:, None, :], axis=2).astype(jnp.float32)
    masked = panel_front * member[:, :, None]
    columns = [None] * PANELS
    inverse_table = {}
    for k in reversed(range(PANELS)):
        later_panels = list(range(k + 1, PANELS))
        direct = product(front_inverse, masked[k])
        for j in later_panels:
            direct = direct + product(columns[j], panel_cross[j, k])
        columns[k] = -member[k][:, None] * direct
        diag_block = diag_inverse[k] - inner(masked[k], columns[k])
        for j in later_panels:
            running = inner(columns[j], masked[k])
            for i in later_panels:
                running = running + product(inverse_table[(j, i)], panel_cross[i, k])
            cross_inv = -running
            inverse_table[(j, k)] = cross_inv
            inverse_table[(k, j)] = cross_inv.T
            diag_block = diag_block - inner(panel_cross[j, k], cross_inv)
        inverse_table[(k, k)] = diag_block
    panel_inverse = jnp.stack([jnp.stack([inverse_table[(j, k)] for k in range(PANELS)]) for j in range(PANELS)])
    return jnp.stack(columns), panel_inverse
```

```python
import jax
import jax.numpy as jnp
from jax import lax
from jax.sharding import PartitionSpec as P

HIGH = lax.Precision.HIGH


def product(left, right):
    return jnp.dot(left, right, precision=HIGH, preferred_element_type=jnp.float32)


def inner(left, right):
    return jnp.einsum(
        "ri,rj->ij", left, right, precision=HIGH, preferred_element_type=jnp.float32
    )


def shards(front_inverse, panel_front, panel_cross, diag_inverse, pattern):
    rows, cols = lax.axis_size("row"), lax.axis_size("col")
    row_index, col_index = lax.axis_index("row"), lax.axis_index("col")
    loc_rows, loc_cols = front_inverse.shape
    panels, _, width = panel_front.shape
    own = loc_cols // rows
    ids = (row_index * loc_rows + jnp.arange(loc_rows, dtype=jnp.int32)) // width
    member = jnp.any(ids[None, :, None] == pattern[:, None, :], axis=2).astype(jnp.float32)
    masked = panel_front * member[:, :, None]
    partial = jnp.einsum(
        "rc,krb->kcb", front_inverse, masked, precision=HIGH, preferred_element_type=jnp.float32
    )
    direct = lax.psum_scatter(partial, "row", scatter_dimension=1, tiled=True)
    placed = [(i, i % rows * cols + i // rows) for i in range(rows * cols)]
    own_panel = lax.dynamic_slice_in_dim(masked, col_index * own, own, 1)
    own_panel = lax.ppermute(own_panel, ("row", "col"), placed)
    block = (col_index * loc_cols + row_index * own) // width
    own_member = jnp.any(pattern == block, axis=1).astype(jnp.float32)
    columns = [None] * panels
    table = {}
    for k in reversed(range(panels)):
        value = direct[k]
        for j in range(k + 1, panels):
            value = value + product(columns[j], panel_cross[j, k])
        columns[k] = -own_member[k] * value
    pairs = [(j, k) for k in range(panels) for j in range(k, panels)]
    grams = lax.psum(jnp.stack([inner(columns[j], own_panel[k]) for j, k in pairs]), ("row", "col"))
    grams = {pair: grams[i] for i, pair in enumerate(pairs)}
    for k in reversed(range(panels)):
        later = range(k + 1, panels)
        diag_block = diag_inverse[k] - grams[k, k].T
        for j in later:
            running = grams[j, k]
            for i in later:
                running = running + product(table[j, i], panel_cross[i, k])
            table[j, k] = -running
            table[k, j] = -running.T
            diag_block = diag_block + inner(panel_cross[j, k], running)
        table[k, k] = diag_block
    panel_inverse = jnp.stack(
        [jnp.stack([table[j, k] for k in range(panels)]) for j in range(panels)]
    )
    back = [(b, a) for a, b in placed]
    return lax.ppermute(jnp.stack(columns), ("row", "col"), back), panel_inverse


def solution(mesh):
    in_specs = (P("row", "col"), P(None, "row", None), P(), P(), P())
    out_specs = (P(None, ("row", "col"), None), P())
    return jax.shard_map(shards, mesh=mesh, in_specs=in_specs, out_specs=out_specs, check_vma=False)
```

```python
import jax
import jax.numpy as jnp
from jax import lax
from jax.experimental import pallas as pl
from jax.experimental.pallas import tpu as pltpu
from jax.sharding import PartitionSpec as P

MESH = pl.DeviceIdType.MESH
F32, BF16 = jnp.float32, jnp.bfloat16
W = 256
PANELS = 4
PAIRS = [(j, k) for k in range(PANELS) for j in range(k + 1, PANELS)]
AT = {pair: i for i, pair in enumerate(PAIRS)}


def split(value):
    high = value.astype(BF16)
    return high, (value - high.astype(F32)).astype(BF16)


def dot(left, right):
    return jnp.dot(left, right, preferred_element_type=F32)


def dot3(left, right):
    return dot(left[0], right[0]) + dot(left[1], right[0]) + dot(left[0], right[1])


class Scratch:
    def __init__(self):
        self.names, self.shapes = [], []

    def add(self, name, shape, dtype=F32):
        self.names.append(name)
        self.shapes.append(pltpu.VMEM(shape, dtype))


def scratch():
    s = Scratch()
    s.add("m32", (PANELS, 2048, W))
    s.add("f32", (4, 2048, W))
    s.add("fh", (4, 2048, W), BF16)
    s.add("fl", (4, 2048, W), BF16)
    s.add("mh", (2, W, 2048), BF16)
    s.add("ml", (2, W, 2048), BF16)
    s.add("part", (PANELS, 4, 2, W, 128))
    s.add("sib", (PANELS, 4, W, 128))
    s.add("chip", (PANELS, 4, W, 128))
    s.add("r1", (PANELS, 2, 128, 128))
    s.add("r2", (PANELS, 2, W, 128))
    s.add("cols", (PANELS, 128, W))
    s.add("ch", (PANELS, 128, W), BF16)
    s.add("cl", (PANELS, 128, W), BF16)
    s.add("placed", (PANELS, 128, W))
    s.add("oh", (PANELS, W, 128), BF16)
    s.add("ol", (PANELS, W, 128), BF16)
    s.add("x32", (len(PAIRS), W, W))
    for name in ("xh", "xl", "xth", "xtl"):
        s.add(name, (len(PAIRS), W, W), BF16)
    s.add("diag", (PANELS, W, W))
    for p in range(PANELS):
        n = p + 1
        s.add(f"g{p}", (2, 4, 4, n, 8, W))
        s.add(f"gs{p}", (4, 4, n, 8, W))
        s.add(f"ga{p}", (3, 4, n, 8, W))
        s.add(f"gb{p}", (3, n, 8, W))
        s.add(f"gx{p}", (4, n, 8, W))
        s.add(f"res{p}", (2, 4, 4, n, 8, W))
    s.add("inv", (PANELS, PANELS, W, W))
    s.add("invt", (PANELS, W, W))
    s.add("pre", (W, W))
    return s


REMOTE = 128
LOCAL = 64


def kernel(names, f_hbm, m_hbm, x_hbm, diag_hbm, pat_ref, cols_hbm, inv_hbm, *refs):
    v = dict(zip(names, refs))
    send_sem, recv_sem, local_sem = refs[len(names):]
    row, col = lax.axis_index("row"), lax.axis_index("col")
    x, core = row // 2, row % 2
    y, z = col // 4, col % 4

    def at(x, y, z, core):
        return ((x % 4) * 2 + core, (y % 4) * 4 + z % 4)

    sibling = at(x, y, z, 1 - core)
    x_peer = [at(x + s, y, z, core) for s in range(4)]
    a_me, b_me = y + (z - y) * core, z + (y - z) * core
    a_peer = [at(x, y + s * (1 - core), z + s * core, core) for s in range(4)]
    b_peer = [at(x, y + s * core, z + s * (1 - core), core) for s in range(4)]
    to = col * 8 + row
    place = (to // 16, to % 16)
    here = row * 16 + col
    source = (here % 8, here // 8)
    stays = to == here

    counts = {"remote": 0, "local": 0}
    pending = []

    def remote(src, dst, device):
        i = counts["remote"]
        counts["remote"] += 1
        return pltpu.make_async_remote_copy(
            src, dst, send_sem.at[i], recv_sem.at[i], device_id=device, device_id_type=MESH
        )

    def local(src, dst):
        i = counts["local"]
        counts["local"] += 1
        return pltpu.make_async_copy(src, dst, local_sem.at[i])

    def send(src, dst, device):
        copy = remote(src, dst, device)
        copy.start()
        pending.append(copy.wait_send)
        return copy

    xs = [x + 2, x + 1, x + 3, x]
    m_copy = [local(m_hbm.at[p], v["m32"].at[p]) for p in range(PANELS)]
    f_copy = []
    for t in range(4):
        first = pl.multiple_of((xs[t] % 4) * W, W)
        f_copy.append(local(f_hbm.at[:, pl.ds(first, W)], v["f32"].at[t]))
    x_copy = [local(x_hbm.at[j, k], v["x32"].at[AT[j, k]]) for j, k in PAIRS]
    diag_copy = local(diag_hbm, v["diag"])
    for copy in [m_copy[3], *f_copy, m_copy[2], *x_copy, m_copy[1], m_copy[0], diag_copy]:
        copy.start()

    barrier = pltpu.get_barrier_semaphore()
    for device in [sibling, *x_peer[1:], *a_peer[1:], *b_peer[1:]]:
        pl.semaphore_signal(barrier, inc=1, device_id=device, device_id_type=MESH)

    @pl.when(jnp.logical_not(stays))
    def _():
        pl.semaphore_signal(barrier, inc=1, device_id=source, device_id_type=MESH)

    pattern = pat_ref[...]

    def member(block):
        return jnp.max(jnp.where(pattern == block, 1.0, 0.0), axis=1, keepdims=True)

    inside = [member(row * 8 + b) for b in range(8)]
    inside_placed = member(row * 8 + col // 2)
    inside_summed = member(col * 4 + row // 2)

    def prep(p):
        m_copy[p].wait()
        for b in range(8):
            block = v["m32"][p, b * W:(b + 1) * W, :] * inside[b][p:p + 1, :]
            high, low = split(block.T)
            v["mh"][p % 2, :, b * W:(b + 1) * W] = high
            v["ml"][p % 2, :, b * W:(b + 1) * W] = low

    def prep_placed(p):
        rows = v["m32"][p, pl.ds(pl.multiple_of(col * 128, 128), 128), :]
        high, low = split((rows * inside_placed[p:p + 1, :]).T)
        v["oh"][p], v["ol"][p] = high, low

    def prep_cross():
        for copy in x_copy:
            copy.wait()
        for i in range(len(PAIRS)):
            block = v["x32"][i]
            v["xh"][i], v["xl"][i] = split(block)
            v["xth"][i], v["xtl"][i] = split(block.T)

    def cross(j, k):
        return v["xh"][AT[j, k]], v["xl"][AT[j, k]]

    def cross_t(j, k):
        return v["xth"][AT[j, k]], v["xtl"][AT[j, k]]

    sib_copy, r1_copy, r2_copy, place_copy = {}, {}, {}, {}

    def tile(p, t):
        if p == 3:
            f_copy[t].wait()
            v["fh"][t], v["fl"][t] = split(v["f32"][t])
        d = dot3((v["mh"][p % 2], v["ml"][p % 2]), (v["fh"][t], v["fl"][t]))
        v["part"][p, t, 0] = d[:, :128]
        v["part"][p, t, 1] = d[:, 128:]
        if p == 3 and t == 0:
            pl.semaphore_wait(barrier, jnp.where(stays, 10, 11))

        sib_copy[p, t] = send(v["part"].at[p, t, 1 - core], v["sib"].at[p, t], sibling)

    def handle(p, t):
        sib_copy[p, t].wait_recv()
        chip = v["chip"].at[p, t]
        chip[...] = v["part"][p, t, core] + v["sib"][p, t]
        if t == 0:
            r1_copy[p, 0] = send(chip.at[:128], v["r1"].at[p, 0], x_peer[1])
            r1_copy[p, 1] = send(chip.at[128:], v["r1"].at[p, 1], x_peer[3])
        if t == 1:
            r2_copy[p, 1] = send(chip.at[128:], v["r2"].at[p, 0, 128:], x_peer[1])
        if t == 2:
            r2_copy[p, 2] = send(chip.at[:128], v["r2"].at[p, 1, :128], x_peer[3])

    def combine(p):
        r1_copy[p, 0].wait_recv()
        chip = v["chip"].at[p, 1, :128]
        chip[...] += v["r1"][p, 0]
        r2_copy[p, 0] = send(chip, v["r2"].at[p, 0, :128], x_peer[1])
        r1_copy[p, 1].wait_recv()
        chip = v["chip"].at[p, 2, 128:]
        chip[...] += v["r1"][p, 1]
        r2_copy[p, 3] = send(chip, v["r2"].at[p, 1, 128:], x_peer[3])

    def final(p):
        for i in range(4):
            r2_copy[p, i].wait_recv()
        d = (v["chip"][p, 3] + v["r2"][p, 0] + v["r2"][p, 1]).T
        for j in range(p + 1, PANELS):
            d = d + dot3((v["ch"][j], v["cl"][j]), cross(j, p))
        c = -inside_summed[p:p + 1, :] * d
        v["cols"][p] = c
        if p > 0:
            v["ch"][p], v["cl"][p] = split(c)
        copy = remote(v["cols"].at[p], v["placed"].at[p], place)
        place_copy[p] = copy

        @pl.when(jnp.logical_not(stays))
        def _():
            copy.start()

        @pl.when(stays)
        def _():
            v["placed"][p] = v["cols"][p]

        def finish():
            @pl.when(jnp.logical_not(stays))
            def _():
                copy.wait_send()

        pending.append(finish)

    core_copy, a_copy, b_copy, gx_copy, back = {}, {}, {}, {}, {}
    out_copy = []

    def gram(p):
        @pl.when(jnp.logical_not(stays))
        def _():
            place_copy[p].wait_recv()

        out = local(v["placed"].at[p], cols_hbm.at[p])
        out.start()
        out_copy.append(out)
        c = split(v["placed"][p])
        for k in range(p + 1):
            value = dot3((v["oh"][k], v["ol"][k]), c)
            v[f"g{p}"][:, :, :, k] = value.reshape(2, 4, 4, 8, W)
        core_copy[p] = send(v[f"g{p}"].at[1 - core], v[f"gs{p}"], sibling)

    def reduce_a(p):
        core_copy[p].wait_recv()
        g = v[f"g{p}"].at[core]
        g[...] += v[f"gs{p}"][...]
        for s in range(1, 4):
            a_copy[p, s] = send(g.at[(a_me + s) % 4], v[f"ga{p}"].at[s - 1], a_peer[s])

    def reduce_b(p):
        g = v[f"g{p}"].at[core, a_me]
        for s in range(1, 4):
            a_copy[p, s].wait_recv()
        g[...] += v[f"ga{p}"][0] + v[f"ga{p}"][1] + v[f"ga{p}"][2]
        for s in range(1, 4):
            b_copy[p, s] = send(g.at[(b_me + s) % 4], v[f"gb{p}"].at[s - 1], b_peer[s])

    def reduce_x(p):
        for s in range(1, 4):
            b_copy[p, s].wait_recv()
        gb, gx = v[f"gb{p}"], v[f"gx{p}"]
        gx[x] = v[f"g{p}"][core, a_me, b_me] + gb[0] + gb[1] + gb[2]
        for s in range(1, 4):
            gx_copy[p, s] = send(gx.at[x], gx.at[x], x_peer[s])

    def gather_b(p):
        for s in range(1, 4):
            gx_copy[p, s].wait_recv()
        gx, res = v[f"gx{p}"], v[f"res{p}"].at[core, a_me, b_me]
        res[...] = (gx[0] + gx[1]) + (gx[2] + gx[3])
        for s in range(1, 4):
            back[p, "b", s] = send(res, res, b_peer[s])

    def gather_a(p):
        for s in range(1, 4):
            back[p, "b", s].wait_recv()
        res = v[f"res{p}"].at[core, a_me]
        for s in range(1, 4):
            back[p, "a", s] = send(res, res, a_peer[s])

    def gather_core(p):
        for s in range(1, 4):
            back[p, "a", s].wait_recv()
        res = v[f"res{p}"].at[core]
        back[p, "core"] = send(res, res, sibling)

    def put(j, k):
        copy = local(v["inv"].at[j, k], inv_hbm.at[j, k])
        copy.start()
        out_copy.append(copy)

    def block(p, k):
        return v[f"res{p}"][:, :, :, k].reshape(W, W)

    def cross_inverse(k):
        later = list(range(k + 1, PANELS))
        total = v["diag"][k]
        for j in later:
            running = block(j, k)
            for i in later:
                right = v["invt"][j] if i == j else v["inv"][i, j]
                running = running + dot3(cross_t(i, k), split(right))
            v["inv"][k, j] = -running
            v["inv"][j, k] = -running.T
            total = total + dot3(cross_t(j, k), split(running.T))
            put(k, j)
            put(j, k)
        v["pre"][...] = total

    def diagonal(k):
        back[k, "core"].wait_recv()
        value = v["pre"][...] - block(k, k)
        v["inv"][k, k] = value
        put(k, k)
        if k > 0:
            v["invt"][k] = value.T
            cross_inverse(k - 1)

    events = []

    def event(time, step, *args):
        events.append((time, len(events), step, args))

    step_us = 0.9
    for p in reversed(range(PANELS)):
        begin = 2.0 + (3 - p) * 4 * step_us
        event(begin - (0.5 if p == 3 else 1.5 * step_us), prep, p)
        for t in range(4):
            event(begin + t * step_us, tile, p, t)
            event(begin + (t + 2) * step_us + 0.3, handle, p, t)
        event(begin + 5 * step_us + 0.4, combine, p)
        when = 11.0 + (3 - p) * 4.5
        event(when, final, p)
        event(when + 2.0, gram, p)
        event(when + 3.5, reduce_a, p)
        event(when + 5.5, reduce_b, p)
        event(when + 7.0, reduce_x, p)
        event(when + 8.2, gather_b, p)
        event(when + 9.5, gather_a, p)
        event(when + 11.5, gather_core, p)
        event(when + 12.5, diagonal, p)
    event(7.5, prep_cross)
    for p in range(PANELS):
        event(12.5 + 0.1 * p, prep_placed, p)

    def prep_diag():
        diag_copy.wait()
        v["pre"][...] = v["diag"][3]

    event(12.9, prep_diag)
    for time, _, step, args in sorted(events, key=lambda e: (e[0], e[1])):
        step(*args)
    for finish in pending:
        finish()
    for copy in out_copy:
        copy.wait()


def shards(front_inverse, panel_front, panel_cross, diag_inverse, pattern):
    s = scratch()
    hbm = pl.BlockSpec(memory_space=pl.ANY)

    def body(*refs):
        kernel(s.names, *refs)

    return pl.pallas_call(
        body,
        out_shape=(
            jax.ShapeDtypeStruct((PANELS, 128, W), F32),
            jax.ShapeDtypeStruct((PANELS, PANELS, W, W), F32),
        ),
        in_specs=[hbm] * 4 + [pl.BlockSpec(memory_space=pltpu.VMEM)],
        out_specs=(hbm, hbm),
        scratch_shapes=s.shapes + [
            pltpu.SemaphoreType.DMA((REMOTE,)),
            pltpu.SemaphoreType.DMA((REMOTE,)),
            pltpu.SemaphoreType.DMA((LOCAL,)),
        ],
        compiler_params=pltpu.CompilerParams(
            collective_id=0, has_side_effects=True, vmem_limit_bytes=62 * 2**20
        ),
        cost_estimate=pl.CostEstimate(
            flops=3 * 2 * 2048 * 1024 * 1024, bytes_accessed=22 * 2**20, transcendentals=0
        ),
    )(front_inverse, panel_front, panel_cross, diag_inverse, pattern)


def solution(mesh):
    in_specs = (P("row", "col"), P(None, "row", None), P(), P(), P())
    out_specs = (P(None, ("row", "col"), None), P())
    return jax.shard_map(shards, mesh=mesh, in_specs=in_specs, out_specs=out_specs, check_vma=False)
```

```python
import jax
import jax.numpy as jnp
from jax import lax
from jax.experimental import pallas as pl
from jax.experimental.pallas import tpu as pltpu
from jax.sharding import PartitionSpec as P

MESH = pl.DeviceIdType.MESH
F32, BF16 = jnp.float32, jnp.bfloat16
W = 256
PANELS = 4
PAIRS = [(j, k) for k in range(PANELS) for j in range(k + 1, PANELS)]
AT = {pair: i for i, pair in enumerate(PAIRS)}


def split(value):
    high = value.astype(BF16)
    return high, (value - high.astype(F32)).astype(BF16)


def dot(left, right):
    return jnp.dot(left, right, preferred_element_type=F32)


def dot3(left, right):
    return dot(left[0], right[0]) + dot(left[1], right[0]) + dot(left[0], right[1])


class Scratch:
    def __init__(self):
        self.names, self.shapes = [], []

    def add(self, name, shape, dtype=F32):
        self.names.append(name)
        self.shapes.append(pltpu.VMEM(shape, dtype))


def scratch():
    s = Scratch()
    s.add("m32", (PANELS, 2048, W))
    s.add("f32", (4, 2048, W))
    s.add("fh", (4, 2048, W), BF16)
    s.add("fl", (4, 2048, W), BF16)
    s.add("mh", (2, W, 2048), BF16)
    s.add("ml", (2, W, 2048), BF16)
    s.add("part", (PANELS, 4, 2, W, 128))
    s.add("sib", (PANELS, 4, W, 128))
    s.add("chip", (PANELS, 4, W, 128))
    s.add("r1", (PANELS, 2, 128, 128))
    s.add("r2", (PANELS, 2, W, 128))
    s.add("cols", (PANELS, 128, W))
    s.add("ch", (PANELS, 128, W), BF16)
    s.add("cl", (PANELS, 128, W), BF16)
    s.add("own", (PANELS, 128, W))
    s.add("midz", (PANELS, 128, W))
    s.add("midy", (PANELS, 128, W))
    s.add("oh", (PANELS, W, 128), BF16)
    s.add("ol", (PANELS, W, 128), BF16)
    s.add("x32", (len(PAIRS), W, W))
    for name in ("xh", "xl", "xth", "xtl"):
        s.add(name, (len(PAIRS), W, W), BF16)
    s.add("diag", (PANELS, W, W))
    for p in range(PANELS):
        n = p + 1
        s.add(f"g{p}", (2, 4, 4, n, 8, W))
        s.add(f"gs{p}", (4, 4, n, 8, W))
        s.add(f"ga{p}", (3, 4, n, 8, W))
        s.add(f"gb{p}", (3, n, 8, W))
        s.add(f"gx{p}", (4, n, 8, W))
        s.add(f"res{p}", (2, 4, 4, n, 8, W))
    s.add("invt", (PANELS, W, W))
    s.add("pre", (W, W))
    return s


REMOTE = 192
VMEM_LIMIT = 58 * 2**20
ORDER = [
    ("prep", 3), ("tile", 3, 0), ("tile", 3, 1), ("tile", 3, 2), ("handle", 3, 0), ("tile", 3, 3),
    ("handle", 3, 2), ("tile", 2, 0), ("tile", 2, 1), ("handle", 3, 1), ("handle", 2, 0), ("tile", 2, 2),
    ("tile", 2, 3), ("tile", 1, 0), ("combine", 3), ("handle", 2, 2), ("cross",), ("diag",), ("handle", 2, 1),
    ("handle", 1, 0), ("own", 2), ("tile", 1, 1), ("own", 1), ("tile", 1, 2), ("combine", 2), ("own", 3),
    ("handle", 3, 3), ("own", 0), ("final", 3), ("pz", 3), ("handle", 1, 1), ("tile", 1, 3), ("handle", 2, 3),
    ("handle", 1, 2), ("combine", 1), ("ra", 3), ("tile", 0, 0), ("final", 2), ("pz", 2), ("handle", 0, 0),
    ("py", 3), ("tile", 0, 1), ("tile", 0, 2), ("ra", 2), ("handle", 1, 3), ("handle", 0, 1), ("handle", 0, 2),
    ("rb", 3), ("combine", 0), ("final", 1), ("pz", 1), ("py", 2), ("tile", 0, 3), ("ra", 1), ("rb", 2),
    ("handle", 0, 3), ("rx", 3), ("final", 0), ("pz", 0), ("py", 1), ("px", 3), ("ra", 0), ("rb", 1), ("rx", 2),
    ("gb", 3), ("py", 0), ("rx", 1), ("rb", 0), ("gb", 2), ("px", 2), ("ga", 3), ("rx", 0), ("gb", 1), ("ga", 2),
    ("px", 0), ("gb", 0), ("gc", 3), ("ga", 1), ("ga", 0), ("settle",), ("px", 1), ("inv", 3), ("gc", 2),
    ("gc", 1), ("inv", 2), ("gc", 0), ("inv", 1), ("inv", 0),
]
LOCAL = 64


def kernel(names, f_hbm, m_hbm, x_hbm, diag_hbm, pat_ref, cols_out, inv_out, *refs):
    v = dict(zip(names, refs))
    send_sem, recv_sem, local_sem = refs[len(names):]
    row, col = lax.axis_index("row"), lax.axis_index("col")
    x, core = row // 2, row % 2
    y, z = col // 4, col % 4

    def at(x, y, z, core):
        return ((x % 4) * 2 + core, (y % 4) * 4 + z % 4)

    sibling = at(x, y, z, 1 - core)
    x_peer = [at(x + s, y, z, core) for s in range(4)]
    a_me, b_me = y + (z - y) * core, z + (y - z) * core
    a_peer = [at(x, y + s * (1 - core), z + s * core, core) for s in range(4)]
    b_peer = [at(x, y + s * core, z + s * (1 - core), core) for s in range(4)]
    chunk = (x + y + z) % 4
    to = col * 8 + 2 * chunk + core
    place = (to // 16, to % 16)
    stays = to == row * 16 + col
    rows_c, rows_k = (row * 16 + col) // 8, (row * 16 + col) % 8
    owner = at(rows_k // 2 - rows_c // 4 - rows_c % 4 + 8, rows_c // 4, rows_c % 4, rows_k % 2)
    to_z = at(x, y, chunk % 2 * 2 + core, z // 2)
    to_z_stays = (to_z[0] == row) & (to_z[1] == col)
    z_was = 2 * core + (z // 2 + x + y) % 2
    to_z_source = at(x, y, z_was, z % 2)
    y_next = z_was % 2 * 2 + (x + y + z_was) % 4 // 2
    to_y = at(x, y_next, z, core)
    x_next = (col % 8 // 2 - x - 2 * core - col // 8 + 8) % 4
    to_x = at(x_next, y, z, core)

    counts = {"remote": 0, "local": 0}
    pending = []

    def remote(src, dst, device):
        i = counts["remote"]
        counts["remote"] += 1
        return pltpu.make_async_remote_copy(
            src, dst, send_sem.at[i], recv_sem.at[i], device_id=device, device_id_type=MESH
        )

    def local(src, dst):
        i = counts["local"]
        counts["local"] += 1
        return pltpu.make_async_copy(src, dst, local_sem.at[i])

    def send(src, dst, device):
        copy = remote(src, dst, device)
        copy.start()
        pending.append(copy.wait_send)
        return copy

    xs = [x + 2, x + 1, x + 3, x]
    m_copy = [local(m_hbm.at[p], v["m32"].at[p]) for p in range(PANELS)]
    f_copy = []
    for t in range(4):
        first = pl.multiple_of(((xs[t] + y + z) % 4) * W, W)
        f_copy.append(local(f_hbm.at[:, pl.ds(first, W)], v["f32"].at[t]))
    x_copy = [local(x_hbm.at[j, k], v["x32"].at[AT[j, k]]) for j, k in PAIRS]
    diag_copy = local(diag_hbm, v["diag"])
    for copy in [m_copy[3], *f_copy, m_copy[2], *x_copy, m_copy[1], m_copy[0], diag_copy]:
        copy.start()

    barrier = pltpu.get_barrier_semaphore()
    for device in [sibling, *x_peer[1:], *a_peer[1:], *b_peer[1:]]:
        pl.semaphore_signal(barrier, inc=1, device_id=device, device_id_type=MESH)

    @pl.when(jnp.logical_not(stays))
    def _():
        pl.semaphore_signal(barrier, inc=1, device_id=place, device_id_type=MESH)

    @pl.when(jnp.logical_not(to_z_stays))
    def _():
        pl.semaphore_signal(barrier, inc=1, device_id=to_z_source, device_id_type=MESH)

    pattern = pat_ref[...]

    def member(block):
        return jnp.max(jnp.where(pattern == block, 1.0, 0.0), axis=1, keepdims=True)

    inside = [member(row * 8 + b) for b in range(8)]
    inside_summed = member(col * 4 + chunk)

    def prep(p, blocks):
        if blocks[0] == 0:
            m_copy[p].wait()
        for b in blocks:
            block = v["m32"][p, b * W:(b + 1) * W, :] * inside[b][p:p + 1, :]
            high, low = split(block.T)
            v["mh"][p % 2, :, b * W:(b + 1) * W] = high
            v["ml"][p % 2, :, b * W:(b + 1) * W] = low

    own_copy = {}

    def enter():
        pl.semaphore_wait(barrier, 10 + jnp.where(stays, 0, 1) + jnp.where(to_z_stays, 0, 1))
        rows = pl.ds(pl.multiple_of(col * 128, 128), 128)
        for p in reversed(range(PANELS)):
            own_copy[p] = remote(m_hbm.at[p, rows], v["own"].at[p], owner)

        @pl.when(jnp.logical_not(stays))
        def _():
            for copy in own_copy.values():
                copy.start()

        @pl.when(stays)
        def _():
            for p in range(PANELS):
                copy = local(m_hbm.at[p, rows], v["own"].at[p])
                copy.start()
                copy.wait()

    def prep_own(p):
        @pl.when(jnp.logical_not(stays))
        def _():
            own_copy[p].wait()

        high, low = split((v["own"][p] * inside_summed[p:p + 1, :]).T)
        v["oh"][p], v["ol"][p] = high, low

    def prep_cross():
        for copy in x_copy:
            copy.wait()
        for i in range(len(PAIRS)):
            block = v["x32"][i]
            v["xh"][i], v["xl"][i] = split(block)
            v["xth"][i], v["xtl"][i] = split(block.T)

    def cross(j, k):
        return v["xh"][AT[j, k]], v["xl"][AT[j, k]]

    def cross_t(j, k):
        return v["xth"][AT[j, k]], v["xtl"][AT[j, k]]

    sib_copy, r1_copy, r2_copy, place_copy = {}, {}, {}, {}
    core_copy, a_copy, b_copy, gx_copy, back = {}, {}, {}, {}, {}
    last = []

    def tile(p, t):
        if p == 3:
            f_copy[t].wait()
            v["fh"][t], v["fl"][t] = split(v["f32"][t])
        if p > 0:
            prep(p - 1, (2 * t, 2 * t + 1))
        d = dot3((v["mh"][p % 2], v["ml"][p % 2]), (v["fh"][t], v["fl"][t]))
        v["part"][p, t, 0] = d[:, :128]
        v["part"][p, t, 1] = d[:, 128:]
        if (p, t) == (3, 0):
            enter()
        sib_copy[p, t] = send(v["part"].at[p, t, 1 - core], v["sib"].at[p, t], sibling)

    def handle(p, t):
        sib_copy[p, t].wait_recv()
        chip = v["chip"].at[p, t]
        chip[...] = v["part"][p, t, core] + v["sib"][p, t]
        if t == 0:
            r1_copy[p, 0] = send(chip.at[:128], v["r1"].at[p, 0], x_peer[1])
            r1_copy[p, 1] = send(chip.at[128:], v["r1"].at[p, 1], x_peer[3])
        if t == 1:
            r2_copy[p, 1] = send(chip.at[128:], v["r2"].at[p, 0, 128:], x_peer[1])
        if t == 2:
            r2_copy[p, 2] = send(chip.at[:128], v["r2"].at[p, 1, :128], x_peer[3])

    def combine(p):
        r1_copy[p, 0].wait_recv()
        chip = v["chip"].at[p, 1, :128]
        chip[...] += v["r1"][p, 0]
        r2_copy[p, 0] = send(chip, v["r2"].at[p, 0, :128], x_peer[1])
        r1_copy[p, 1].wait_recv()
        chip = v["chip"].at[p, 2, 128:]
        chip[...] += v["r1"][p, 1]
        r2_copy[p, 3] = send(chip, v["r2"].at[p, 1, 128:], x_peer[3])

    def final(p):
        for i in range(4):
            r2_copy[p, i].wait_recv()
        d = (v["chip"][p, 3] + v["r2"][p, 0] + v["r2"][p, 1]).T
        gram(p, p, split(d))
        if p == 0:
            core_copy[p] = send(v["g0"].at[1 - core], v["gs0"], sibling)
        for j in range(p + 1, PANELS):
            d = d + dot3((v["ch"][j], v["cl"][j]), cross(j, p))
        c = -inside_summed[p:p + 1, :] * d
        v["cols"][p] = c
        if p > 0:
            pair = split(c)
            v["ch"][p], v["cl"][p] = pair
            for k in range(p):
                gram(p, k, pair)
            core_copy[p] = send(v[f"g{p}"].at[1 - core], v[f"gs{p}"], sibling)

    def move(src, dst, device, here):
        copy, stay = remote(src, dst, device), local(src, dst)

        @pl.when(jnp.logical_not(here))
        def _():
            copy.start()

        @pl.when(here)
        def _():
            stay.start()

        def arrive():
            @pl.when(jnp.logical_not(here))
            def _():
                copy.wait_recv()

            @pl.when(here)
            def _():
                stay.wait()

        def sent():
            @pl.when(jnp.logical_not(here))
            def _():
                copy.wait_send()

        last.append(sent)
        return arrive

    def place_z(p):
        place_copy[p] = move(v["cols"].at[p], v["midz"].at[p], to_z, to_z_stays)

    def place_y(p):
        place_copy[p]()
        place_copy[p] = move(v["midz"].at[p], v["midy"].at[p], to_y, y_next == y)

    def place_x(p):
        place_copy[p]()
        place_copy[p] = move(v["midy"].at[p], cols_out.at[p], to_x, x_next == x)

    def gram(p, k, right):
        value = dot3((v["oh"][k], v["ol"][k]), right)
        v[f"g{p}"][:, :, :, k] = value.reshape(2, 4, 4, 8, W)

    def reduce_a(p):
        core_copy[p].wait_recv()
        g = v[f"g{p}"].at[core]
        g[...] += v[f"gs{p}"][...]
        for s in range(1, 4):
            a_copy[p, s] = send(g.at[(a_me + s) % 4], v[f"ga{p}"].at[s - 1], a_peer[s])

    def reduce_b(p):
        g = v[f"g{p}"].at[core, a_me]
        for s in range(1, 4):
            a_copy[p, s].wait_recv()
        g[...] += v[f"ga{p}"][0] + v[f"ga{p}"][1] + v[f"ga{p}"][2]
        for s in range(1, 4):
            b_copy[p, s] = send(g.at[(b_me + s) % 4], v[f"gb{p}"].at[s - 1], b_peer[s])

    def reduce_x(p):
        for s in range(1, 4):
            b_copy[p, s].wait_recv()
        gb, gx = v[f"gb{p}"], v[f"gx{p}"]
        gx[x] = v[f"g{p}"][core, a_me, b_me] + gb[0] + gb[1] + gb[2]
        for s in range(1, 4):
            gx_copy[p, s] = send(gx.at[x], gx.at[x], x_peer[s])

    def gather_b(p):
        for s in range(1, 4):
            gx_copy[p, s].wait_recv()
        gx, res = v[f"gx{p}"], v[f"res{p}"].at[core, a_me, b_me]
        res[...] = (gx[0] + gx[1]) + (gx[2] + gx[3])
        for s in range(1, 4):
            back[p, "b", s] = send(res, res, b_peer[s])

    def gather_a(p):
        for s in range(1, 4):
            back[p, "b", s].wait_recv()
        res = v[f"res{p}"].at[core, a_me]
        for s in range(1, 4):
            back[p, "a", s] = send(res, res, a_peer[s])

    def gather_core(p):
        for key, copy in back.items():
            if key[:2] == (p, "a"):
                copy.wait_recv()
        res = v[f"res{p}"].at[core]
        back[p, "core"] = send(res, res, sibling)

    def block(p, k):
        return v[f"res{p}"][:, :, :, k].reshape(W, W)

    def cross_inverse(k):
        later = list(range(k + 1, PANELS))
        total = v["diag"][k]
        for j in later:
            running = block(j, k)
            total = total + dot3(split(running), cross(j, k))
            for i in later:
                right = v["invt"][j] if i == j else inv_out[i, j]
                running = running + dot3(cross_t(i, k), split(right))
            inv_out[k, j] = -running
            inv_out[j, k] = -running.T
            total = total + dot3(cross_t(j, k), split(running.T))
        v["pre"][...] = total

    def diagonal(k):
        back[k, "core"].wait_recv()
        value = v["pre"][...] + block(k, k)
        inv_out[k, k] = value
        if k > 0:
            v["invt"][k] = value.T
            cross_inverse(k - 1)

    def start_diag():
        diag_copy.wait()
        v["pre"][...] = v["diag"][3]

    def settle():
        for finish in pending:
            finish()
        pending.clear()

    steps = {
        "prep": lambda p: prep(p, range(8)), "tile": tile, "handle": handle, "combine": combine,
        "own": prep_own, "cross": prep_cross, "diag": start_diag, "final": final, "ra": reduce_a, "rb": reduce_b,
        "rx": reduce_x, "gb": gather_b, "ga": gather_a, "gc": gather_core, "inv": diagonal, "pz": place_z,
        "py": place_y, "px": place_x, "settle": settle,
    }
    for name, *where in ORDER:
        steps[name](*where)
    settle()
    for p in range(PANELS):
        place_copy[p]()
    for finish in last:
        finish()


def copy_kernel(cols_in, inv_in, cols_hbm, inv_hbm, sem):
    copies = [
        pltpu.make_async_copy(cols_in, cols_hbm, sem.at[0]),
        *[pltpu.make_async_copy(inv_in.at[k], inv_hbm.at[k], sem.at[1 + k]) for k in range(PANELS)],
    ]
    for copy in copies:
        copy.start()
    for copy in copies:
        copy.wait()


def shards(front_inverse, panel_front, panel_cross, diag_inverse, pattern):
    s = scratch()
    hbm, vmem = pl.BlockSpec(memory_space=pl.ANY), pl.BlockSpec(memory_space=pltpu.VMEM)
    shapes = (PANELS, 128, W), (PANELS, PANELS, W, W)

    def body(*refs):
        kernel(s.names, *refs)

    held = pl.pallas_call(
        body,
        out_shape=tuple(pltpu.VMEM(shape, F32) for shape in shapes),
        in_specs=[hbm] * 4 + [vmem],
        out_specs=(vmem, vmem),
        scratch_shapes=s.shapes + [
            pltpu.SemaphoreType.DMA((REMOTE,)),
            pltpu.SemaphoreType.DMA((REMOTE,)),
            pltpu.SemaphoreType.DMA((LOCAL,)),
        ],
        compiler_params=pltpu.CompilerParams(
            collective_id=0, has_side_effects=True, vmem_limit_bytes=VMEM_LIMIT
        ),
        cost_estimate=pl.CostEstimate(
            flops=3 * 2 * 2048 * 1024 * 1024, bytes_accessed=22 * 2**20, transcendentals=0
        ),
    )(front_inverse, panel_front, panel_cross, diag_inverse, pattern)
    return pl.pallas_call(
        copy_kernel,
        out_shape=tuple(jax.ShapeDtypeStruct(shape, F32) for shape in shapes),
        in_specs=[vmem, vmem],
        out_specs=(hbm, hbm),
        scratch_shapes=[pltpu.SemaphoreType.DMA((1 + PANELS,))],
        compiler_params=pltpu.CompilerParams(vmem_limit_bytes=8 * 2**20),
    )(*held)


def solution(mesh):
    in_specs = (P("row", "col"), P(None, "row", None), P(), P(), P())
    out_specs = (P(None, ("row", "col"), None), P())
    return jax.shard_map(shards, mesh=mesh, in_specs=in_specs, out_specs=out_specs, check_vma=False)
```

```python
import jax
import jax.numpy as jnp
from jax import lax
from jax.experimental import pallas as pl
from jax.experimental.pallas import tpu as pltpu
from jax.sharding import PartitionSpec as P

MESH = pl.DeviceIdType.MESH
F32, BF16 = jnp.float32, jnp.bfloat16
W = 256
PANELS = 4
PAIRS = [(j, k) for k in range(PANELS) for j in range(k + 1, PANELS)]
AT = {pair: i for i, pair in enumerate(PAIRS)}


def split(value):
    high = value.astype(BF16)
    return high, (value - high.astype(F32)).astype(BF16)


def dot(left, right):
    return jnp.dot(left, right, preferred_element_type=F32)


def dot3(left, right):
    return dot(left[0], right[0]) + dot(left[1], right[0]) + dot(left[0], right[1])


class Scratch:
    def __init__(self):
        self.names, self.shapes = [], []

    def add(self, name, shape, dtype=F32):
        self.names.append(name)
        self.shapes.append(pltpu.VMEM(shape, dtype))


def scratch():
    s = Scratch()
    s.add("m32", (PANELS, 2048, W))
    s.add("f32", (4, 2048, W))
    s.add("fh", (4, 2048, W), BF16)
    s.add("fl", (4, 2048, W), BF16)
    s.add("mh", (W, 2048), BF16)
    s.add("ml", (W, 2048), BF16)
    s.add("part", (PANELS, 4, 2, W, 128))
    s.add("sib", (PANELS, 4, W, 128))
    s.add("chip", (PANELS, 4, W, 128))
    s.add("r1", (PANELS, 2, 128, 128))
    s.add("r2", (PANELS, 2, W, 128))
    s.add("cols", (PANELS, 128, W))
    s.add("ch", (PANELS, 128, W), BF16)
    s.add("cl", (PANELS, 128, W), BF16)
    s.add("own", (PANELS, 128, W))
    s.add("midz", (PANELS, 128, W))
    s.add("midy", (PANELS, 128, W))
    s.add("oh", (PANELS, W, 128), BF16)
    s.add("ol", (PANELS, W, 128), BF16)
    s.add("x32", (len(PAIRS), W, W))
    for name in ("xh", "xl", "xth", "xtl"):
        s.add(name, (len(PAIRS), W, W), BF16)
    s.add("diag", (PANELS, W, W))
    for p in range(PANELS):
        n = p + 1
        s.add(f"g{p}", (2, 4, 4, n, 8, W))
        s.add(f"gs{p}", (4, 4, n, 8, W))
        s.add(f"ga{p}", (3, 4, n, 8, W))
        s.add(f"gb{p}", (3, n, 8, W))
        s.add(f"gx{p}", (4, n, 8, W))
        s.add(f"res{p}", (2, 4, 4, n, 8, W))
    s.add("invt", (PANELS, W, W))
    s.add("pre", (W, W))
    return s


REMOTE = 192
VMEM_LIMIT = 58 * 2**20
BETWEEN = [
    [],
    [],
    [
        ("handle", 3, 0),
    ],
    [
        ("handle", 3, 2),
    ],
    [],
    [
        ("handle", 3, 1), ("handle", 2, 0),
    ],
    [],
    [],
    [
        ("combine", 3), ("handle", 2, 2), ("cross",), ("diag",), ("handle", 2, 1), ("handle", 1, 0),
        ("own", 2),
    ],
    [
        ("own", 1),
    ],
    [
        ("combine", 2), ("own", 3), ("handle", 3, 3), ("own", 0), ("final", 3), ("pz", 3), ("handle", 1, 1),
    ],
    [
        ("handle", 2, 3), ("handle", 1, 2), ("combine", 1), ("ra", 3),
    ],
    [
        ("final", 2), ("pz", 2), ("handle", 0, 0), ("py", 3),
    ],
    [],
    [
        ("ra", 2), ("handle", 1, 3), ("handle", 0, 1), ("handle", 0, 2), ("rb", 3), ("combine", 0),
        ("final", 1), ("pz", 1), ("py", 2),
    ],
    [],
]
AFTER = [
    ("ra", 1), ("rb", 2), ("handle", 0, 3), ("rx", 3), ("final", 0), ("pz", 0), ("py", 1), ("px", 3),
    ("ra", 0), ("rb", 1), ("rx", 2), ("gb", 3), ("py", 0), ("rx", 1), ("rb", 0), ("gb", 2), ("px", 2),
    ("ga", 3), ("rx", 0), ("gb", 1), ("ga", 2), ("px", 0), ("gb", 0), ("gc", 3), ("ga", 1), ("ga", 0),
    ("settle",), ("px", 1), ("inv", 3), ("gc", 2), ("gc", 1), ("inv", 2), ("gc", 0), ("inv", 1), ("inv", 0),
]
LOCAL = 64


def kernel(names, f_hbm, m_hbm, x_hbm, diag_hbm, pat_ref, cols_out, inv_out, *refs):
    v = dict(zip(names, refs))
    send_sem, recv_sem, local_sem, sib_send_sem, sib_recv_sem = refs[len(names):]
    row, col = lax.axis_index("row"), lax.axis_index("col")
    x, core = row // 2, row % 2
    y, z = col // 4, col % 4

    def at(x, y, z, core):
        return ((x % 4) * 2 + core, (y % 4) * 4 + z % 4)

    sibling = at(x, y, z, 1 - core)
    x_peer = [at(x + s, y, z, core) for s in range(4)]
    a_me, b_me = y + (z - y) * core, z + (y - z) * core
    a_peer = [at(x, y + s * (1 - core), z + s * core, core) for s in range(4)]
    b_peer = [at(x, y + s * core, z + s * (1 - core), core) for s in range(4)]
    chunk = (x + y + z) % 4
    to = col * 8 + 2 * chunk + core
    place = (to // 16, to % 16)
    stays = to == row * 16 + col
    rows_c, rows_k = (row * 16 + col) // 8, (row * 16 + col) % 8
    owner = at(rows_k // 2 - rows_c // 4 - rows_c % 4 + 8, rows_c // 4, rows_c % 4, rows_k % 2)
    to_z = at(x, y, chunk % 2 * 2 + core, z // 2)
    to_z_stays = (to_z[0] == row) & (to_z[1] == col)
    z_was = 2 * core + (z // 2 + x + y) % 2
    to_z_source = at(x, y, z_was, z % 2)
    y_next = z_was % 2 * 2 + (x + y + z_was) % 4 // 2
    to_y = at(x, y_next, z, core)
    x_next = (col % 8 // 2 - x - 2 * core - col // 8 + 8) % 4
    to_x = at(x_next, y, z, core)

    other = 1 - core
    a_at = [(a_me + s) % 4 for s in range(4)]
    b_at = [(b_me + s) % 4 for s in range(4)]
    own_rows = pl.ds(pl.multiple_of(col * 128, 128), 128)
    away, away_z, y_here, x_here = jnp.logical_not(stays), jnp.logical_not(to_z_stays), y_next == y, x_next == x
    y_away, x_away = jnp.logical_not(y_here), jnp.logical_not(x_here)

    counts = {"remote": 0, "local": 0}
    pending = []

    class Remote:
        def __init__(self, src, dst, device):
            self.what = src, dst, counts["remote"], device
            counts["remote"] += 1

        def copy(self):
            src, dst, i, device = self.what
            return pltpu.make_async_remote_copy(
                src(), dst(), send_sem.at[i], recv_sem.at[i], device_id=device, device_id_type=MESH
            )

        def start(self):
            self.copy().start()

        def wait_recv(self):
            self.copy().wait_recv()

        def wait_send(self):
            self.copy().wait_send()

    class Local:
        def __init__(self, src, dst):
            self.what = src, dst, counts["local"]
            counts["local"] += 1

        def copy(self):
            src, dst, i = self.what
            return pltpu.make_async_copy(src(), dst(), local_sem.at[i])

        def start(self):
            self.copy().start()

        def wait(self):
            self.copy().wait()

    def send(src, dst, device):
        copy = Remote(src, dst, device)
        copy.start()
        pending.append(copy.wait_send)
        return copy

    def part_of(name, *index):
        return lambda: v[name].at[index]

    xs = [x + 2, x + 1, x + 3, x]
    m_copy = [Local(lambda p=p: m_hbm.at[p], part_of("m32", p)) for p in range(PANELS)]
    f_copy = []
    for t in range(4):
        first = pl.multiple_of(((xs[t] + y + z) % 4) * W, W)
        f_copy.append(Local(lambda first=first: f_hbm.at[:, pl.ds(first, W)], part_of("f32", t)))
    x_copy = [Local(lambda j=j, k=k: x_hbm.at[j, k], part_of("x32", AT[j, k])) for j, k in PAIRS]
    diag_copy = Local(lambda: diag_hbm, lambda: v["diag"])
    for copy in [m_copy[3], *f_copy, m_copy[2], *x_copy, m_copy[1], m_copy[0], diag_copy]:
        copy.start()

    barrier = pltpu.get_barrier_semaphore()
    for device in [sibling, *x_peer[1:], *a_peer[1:], *b_peer[1:]]:
        pl.semaphore_signal(barrier, inc=1, device_id=device, device_id_type=MESH)

    @pl.when(jnp.logical_not(stays))
    def _():
        pl.semaphore_signal(barrier, inc=1, device_id=place, device_id_type=MESH)

    @pl.when(jnp.logical_not(to_z_stays))
    def _():
        pl.semaphore_signal(barrier, inc=1, device_id=to_z_source, device_id_type=MESH)

    pattern = pat_ref[...]

    def member(block):
        return jnp.max(jnp.where(pattern == block, 1.0, 0.0), axis=1, keepdims=True)

    inside = [member(row * 8 + b) for b in range(8)]
    inside_summed = member(col * 4 + chunk)

    def prep(p):
        pltpu.make_async_copy(m_hbm.at[p], v["m32"].at[p], local_sem.at[p]).wait()
        for b in range(8):
            keep = inside[b][3:, :]
            for k in range(PANELS - 1):
                keep = jnp.where(p == k, inside[b][k:k + 1, :], keep)
            high, low = split((v["m32"][p, b * W:(b + 1) * W, :] * keep).T)
            v["mh"][:, b * W:(b + 1) * W] = high
            v["ml"][:, b * W:(b + 1) * W] = low

    own_copy = {}

    def enter():
        pl.semaphore_wait(barrier, 10 + jnp.where(stays, 0, 1) + jnp.where(to_z_stays, 0, 1))
        for p in reversed(range(PANELS)):
            own_copy[p] = Remote(lambda p=p: m_hbm.at[p, own_rows], part_of("own", p), owner)

        @pl.when(away)
        def _():
            for copy in own_copy.values():
                copy.start()

        @pl.when(stays)
        def _():
            for p in range(PANELS):
                copy = Local(lambda p=p: m_hbm.at[p, own_rows], part_of("own", p))
                copy.start()
                copy.wait()

    def prep_own(p):
        @pl.when(away)
        def _():
            own_copy[p].wait_recv()
            own_copy[p].wait_send()

        high, low = split((v["own"][p] * inside_summed[p:p + 1, :]).T)
        v["oh"][p], v["ol"][p] = high, low

    def prep_cross():
        for copy in x_copy:
            copy.wait()
        for i in range(len(PAIRS)):
            block = v["x32"][i]
            v["xh"][i], v["xl"][i] = split(block)
            v["xth"][i], v["xtl"][i] = split(block.T)

    def cross(j, k):
        return v["xh"][AT[j, k]], v["xl"][AT[j, k]]

    def cross_t(j, k):
        return v["xth"][AT[j, k]], v["xtl"][AT[j, k]]

    r1_copy, r2_copy, place_copy = {}, {}, {}
    core_copy, a_copy, b_copy, gx_copy, back = {}, {}, {}, {}, {}
    last = []

    def sib_copy(p, t):
        i = (3 - p) * 4 + t
        return pltpu.make_async_remote_copy(
            v["part"].at[p, t, other], v["sib"].at[p, t], sib_send_sem.at[i], sib_recv_sem.at[i],
            device_id=sibling, device_id_type=MESH,
        )

    def tile(step):
        p, t = 3 - step // 4, step % 4

        @pl.when(t == 0)
        def _():
            prep(p)

        @pl.when(step < 4)
        def _():
            pltpu.make_async_copy(v["f32"].at[t], v["f32"].at[t], local_sem.at[PANELS + t]).wait()
            v["fh"][t], v["fl"][t] = split(v["f32"][t])

        d = dot3((v["mh"][...], v["ml"][...]), (v["fh"][t], v["fl"][t]))
        v["part"][p, t, 0] = d[:, :128]
        v["part"][p, t, 1] = d[:, 128:]

        @pl.when(step == 0)
        def _():
            enter()

        sib_copy(p, t).start()

    def handle(p, t):
        sib_copy(p, t).wait_recv()
        chip = v["chip"].at[p, t]
        chip[...] = v["part"][p, t, core] + v["sib"][p, t]
        if t == 0:
            r1_copy[p, 0] = send(part_of("chip", p, 0, pl.ds(0, 128)), part_of("r1", p, 0), x_peer[1])
            r1_copy[p, 1] = send(part_of("chip", p, 0, pl.ds(128, 128)), part_of("r1", p, 1), x_peer[3])
        if t == 1:
            r2_copy[p, 1] = send(part_of("chip", p, 1, pl.ds(128, 128)), part_of("r2", p, 0, pl.ds(128, 128)), x_peer[1])
        if t == 2:
            r2_copy[p, 2] = send(part_of("chip", p, 2, pl.ds(0, 128)), part_of("r2", p, 1, pl.ds(0, 128)), x_peer[3])

    def combine(p):
        r1_copy[p, 0].wait_recv()
        chip = v["chip"].at[p, 1, :128]
        chip[...] += v["r1"][p, 0]
        r2_copy[p, 0] = send(part_of("chip", p, 1, pl.ds(0, 128)), part_of("r2", p, 0, pl.ds(0, 128)), x_peer[1])
        r1_copy[p, 1].wait_recv()
        chip = v["chip"].at[p, 2, 128:]
        chip[...] += v["r1"][p, 1]
        r2_copy[p, 3] = send(part_of("chip", p, 2, pl.ds(128, 128)), part_of("r2", p, 1, pl.ds(128, 128)), x_peer[3])

    def final(p):
        for i in range(4):
            r2_copy[p, i].wait_recv()
        d = (v["chip"][p, 3] + v["r2"][p, 0] + v["r2"][p, 1]).T
        gram(p, p, split(d))
        if p == 0:
            core_copy[p] = send(part_of("g0", other), lambda: v["gs0"], sibling)
        for j in range(p + 1, PANELS):
            d = d + dot3((v["ch"][j], v["cl"][j]), cross(j, p))
        c = -inside_summed[p:p + 1, :] * d
        v["cols"][p] = c
        if p > 0:
            pair = split(c)
            v["ch"][p], v["cl"][p] = pair
            for k in range(p):
                gram(p, k, pair)
            core_copy[p] = send(part_of(f"g{p}", other), lambda: v[f"gs{p}"], sibling)

    def move(src, dst, device, here, away):
        copy, stay = Remote(src, dst, device), Local(src, dst)

        @pl.when(away)
        def _():
            copy.start()

        @pl.when(here)
        def _():
            stay.start()

        def arrive():
            @pl.when(away)
            def _():
                copy.wait_recv()

            @pl.when(here)
            def _():
                stay.wait()

        def sent():
            @pl.when(away)
            def _():
                copy.wait_send()

        last.append(sent)
        return arrive

    def place_z(p):
        place_copy[p] = move(part_of("cols", p), part_of("midz", p), to_z, to_z_stays, away_z)

    def place_y(p):
        place_copy[p]()
        place_copy[p] = move(part_of("midz", p), part_of("midy", p), to_y, y_here, y_away)

    def place_x(p):
        place_copy[p]()
        place_copy[p] = move(part_of("midy", p), lambda: cols_out.at[p], to_x, x_here, x_away)

    def gram(p, k, right):
        value = dot3((v["oh"][k], v["ol"][k]), right)
        v[f"g{p}"][:, :, :, k] = value.reshape(2, 4, 4, 8, W)

    def reduce_a(p):
        core_copy[p].wait_recv()
        g = v[f"g{p}"].at[core]
        g[...] += v[f"gs{p}"][...]
        for s in range(1, 4):
            a_copy[p, s] = send(part_of(f"g{p}", core, a_at[s]), part_of(f"ga{p}", s - 1), a_peer[s])

    def reduce_b(p):
        g = v[f"g{p}"].at[core, a_me]
        for s in range(1, 4):
            a_copy[p, s].wait_recv()
        g[...] += v[f"ga{p}"][0] + v[f"ga{p}"][1] + v[f"ga{p}"][2]
        for s in range(1, 4):
            b_copy[p, s] = send(part_of(f"g{p}", core, a_me, b_at[s]), part_of(f"gb{p}", s - 1), b_peer[s])

    def reduce_x(p):
        for s in range(1, 4):
            b_copy[p, s].wait_recv()
        gb, gx = v[f"gb{p}"], v[f"gx{p}"]
        gx[x] = v[f"g{p}"][core, a_me, b_me] + gb[0] + gb[1] + gb[2]
        for s in range(1, 4):
            gx_copy[p, s] = send(part_of(f"gx{p}", x), part_of(f"gx{p}", x), x_peer[s])

    def gather_b(p):
        for s in range(1, 4):
            gx_copy[p, s].wait_recv()
        gx, res_at = v[f"gx{p}"], part_of(f"res{p}", core, a_me, b_me)
        v[f"res{p}"][core, a_me, b_me] = (gx[0] + gx[1]) + (gx[2] + gx[3])
        for s in range(1, 4):
            back[p, "b", s] = send(res_at, res_at, b_peer[s])

    def gather_a(p):
        for s in range(1, 4):
            back[p, "b", s].wait_recv()
        res_at = part_of(f"res{p}", core, a_me)
        for s in range(1, 4):
            back[p, "a", s] = send(res_at, res_at, a_peer[s])

    def gather_core(p):
        for key, copy in back.items():
            if key[:2] == (p, "a"):
                copy.wait_recv()
        res_at = part_of(f"res{p}", core)
        back[p, "core"] = send(res_at, res_at, sibling)

    def block(p, k):
        return v[f"res{p}"][:, :, :, k].reshape(W, W)

    def cross_inverse(k):
        later = list(range(k + 1, PANELS))
        total = v["diag"][k]
        for j in later:
            running = block(j, k)
            total = total + dot3(split(running), cross(j, k))
            for i in later:
                right = v["invt"][j] if i == j else inv_out[i, j]
                running = running + dot3(cross_t(i, k), split(right))
            inv_out[k, j] = -running
            inv_out[j, k] = -running.T
            total = total + dot3(cross_t(j, k), split(running.T))
        v["pre"][...] = total

    def diagonal(k):
        back[k, "core"].wait_recv()
        value = v["pre"][...] + block(k, k)
        inv_out[k, k] = value
        if k > 0:
            v["invt"][k] = value.T
            cross_inverse(k - 1)

    def start_diag():
        diag_copy.wait()
        v["pre"][...] = v["diag"][3]

    def settle():
        for finish in pending:
            finish()
        pending.clear()

    steps = {
        "handle": handle, "combine": combine, "own": prep_own, "cross": prep_cross, "diag": start_diag,
        "final": final, "ra": reduce_a, "rb": reduce_b, "rx": reduce_x, "gb": gather_b, "ga": gather_a,
        "gc": gather_core, "inv": diagonal, "pz": place_z, "py": place_y, "px": place_x, "settle": settle,
    }

    def take(order):
        for name, *where in order:
            steps[name](*where)

    @pl.loop(0, 16)
    def _(step):
        tile(step)
        for i, order in enumerate(BETWEEN):
            if order:
                pl.when(step == i)(lambda order=order: take(order))

    take(AFTER)
    for p in range(PANELS):
        for t in range(4):
            sib_copy(p, t).wait_send()
    settle()
    for p in range(PANELS):
        place_copy[p]()
    for finish in last:
        finish()


def copy_kernel(cols_in, inv_in, cols_hbm, inv_hbm, sem):
    copies = [
        pltpu.make_async_copy(cols_in, cols_hbm, sem.at[0]),
        *[pltpu.make_async_copy(inv_in.at[k], inv_hbm.at[k], sem.at[1 + k]) for k in range(PANELS)],
    ]
    for copy in copies:
        copy.start()
    for copy in copies:
        copy.wait()


def shards(front_inverse, panel_front, panel_cross, diag_inverse, pattern):
    s = scratch()
    hbm, vmem = pl.BlockSpec(memory_space=pl.ANY), pl.BlockSpec(memory_space=pltpu.VMEM)
    shapes = (PANELS, 128, W), (PANELS, PANELS, W, W)

    def body(*refs):
        kernel(s.names, *refs)

    held = pl.pallas_call(
        body,
        out_shape=tuple(pltpu.VMEM(shape, F32) for shape in shapes),
        in_specs=[hbm] * 4 + [vmem],
        out_specs=(vmem, vmem),
        scratch_shapes=s.shapes + [
            pltpu.SemaphoreType.DMA((REMOTE,)),
            pltpu.SemaphoreType.DMA((REMOTE,)),
            pltpu.SemaphoreType.DMA((LOCAL,)),
            pltpu.SemaphoreType.DMA((16,)),
            pltpu.SemaphoreType.DMA((16,)),
        ],
        compiler_params=pltpu.CompilerParams(
            collective_id=0, has_side_effects=True, vmem_limit_bytes=VMEM_LIMIT
        ),
        cost_estimate=pl.CostEstimate(
            flops=3 * 2 * 2048 * 1024 * 1024, bytes_accessed=22 * 2**20, transcendentals=0
        ),
    )(front_inverse, panel_front, panel_cross, diag_inverse, pattern)
    return pl.pallas_call(
        copy_kernel,
        out_shape=tuple(jax.ShapeDtypeStruct(shape, F32) for shape in shapes),
        in_specs=[vmem, vmem],
        out_specs=(hbm, hbm),
        scratch_shapes=[pltpu.SemaphoreType.DMA((1 + PANELS,))],
        compiler_params=pltpu.CompilerParams(vmem_limit_bytes=8 * 2**20),
    )(*held)


def solution(mesh):
    in_specs = (P("row", "col"), P(None, "row", None), P(), P(), P())
    out_specs = (P(None, ("row", "col"), None), P())
    return jax.shard_map(shards, mesh=mesh, in_specs=in_specs, out_specs=out_specs, check_vma=False)
```

```python
import jax
import jax.numpy as jnp
from jax import lax
from jax.experimental import pallas as pl
from jax.experimental.pallas import tpu as pltpu
from jax.sharding import PartitionSpec as P

MESH = pl.DeviceIdType.MESH
F32, BF16 = jnp.float32, jnp.bfloat16
W = 256
PANELS = 4
PAIRS = [(j, k) for k in range(PANELS) for j in range(k + 1, PANELS)]
AT = {pair: i for i, pair in enumerate(PAIRS)}


def split(value):
    high = value.astype(BF16)
    return high, (value - high.astype(F32)).astype(BF16)


def dot(left, right):
    return jnp.dot(left, right, preferred_element_type=F32)


def dot3(left, right):
    return dot(left[0], right[0]) + dot(left[1], right[0]) + dot(left[0], right[1])


class Scratch:
    def __init__(self):
        self.names, self.shapes = [], []

    def add(self, name, shape, dtype=F32):
        self.names.append(name)
        self.shapes.append(pltpu.VMEM(shape, dtype))


def scratch():
    s = Scratch()
    s.add("m32", (PANELS, 2048, W))
    s.add("f32", (4, 2048, W))
    s.add("fh", (4, 2048, W), BF16)
    s.add("fl", (4, 2048, W), BF16)
    s.add("mh", (W, 2048), BF16)
    s.add("ml", (W, 2048), BF16)
    s.add("part", (PANELS, 4, 2, W, 128))
    s.add("sib", (PANELS, 4, W, 128))
    s.add("chip", (PANELS, 4, W, 128))
    s.add("r1", (PANELS, 2, 128, 128))
    s.add("r2", (PANELS, 2, W, 128))
    s.add("cols", (PANELS, 128, W))
    s.add("ch", (PANELS, 128, W), BF16)
    s.add("cl", (PANELS, 128, W), BF16)
    s.add("own", (PANELS, 128, W))
    s.add("midz", (PANELS, 128, W))
    s.add("midy", (PANELS, 128, W))
    s.add("oh", (PANELS, W, 128), BF16)
    s.add("ol", (PANELS, W, 128), BF16)
    s.add("x32", (len(PAIRS), W, W))
    for name in ("xh", "xl", "xth", "xtl"):
        s.add(name, (len(PAIRS), W, W), BF16)
    s.add("diag", (PANELS, W, W))
    for p in range(PANELS):
        n = p + 1
        s.add(f"g{p}", (2, 4, 4, n, 8, W))
        s.add(f"gs{p}", (4, 4, n, 8, W))
        s.add(f"ga{p}", (3, 4, n, 8, W))
        s.add(f"gb{p}", (3, n, 8, W))
        s.add(f"gx{p}", (4, n, 8, W))
        s.add(f"res{p}", (2, 4, 4, n, 8, W))
    s.add("invt", (PANELS, W, W))
    s.add("pre", (W, W))
    return s


REMOTE = 192
VMEM_LIMIT = 58 * 2**20
BETWEEN = [
    [],
    [],
    [
        ("handle", 3, 0),
    ],
    [],
    [
        ("handle", 3, 3),
    ],
    [
        ("handle", 3, 2), ("handle", 3, 1),
    ],
    [],
    [
        ("handle", 2, 0),
    ],
    [
        ("own", 3), ("combine", 3), ("cross",), ("diag",), ("handle", 1, 0), ("handle", 2, 3),
    ],
    [
        ("handle", 2, 1), ("handle", 2, 2), ("own", 2), ("combine", 2), ("handle", 1, 1),
    ],
    [
        ("own", 1), ("own", 0), ("final", 3), ("pz", 3),
    ],
    [
        ("handle", 1, 2), ("combine", 1), ("ra", 3),
    ],
    [
        ("final", 2), ("pz", 2), ("handle", 0, 0),
    ],
    [
        ("ra", 2),
    ],
    [
        ("rb", 3), ("handle", 0, 1), ("handle", 1, 3), ("py", 3), ("handle", 0, 2), ("combine", 0),
        ("final", 1),
    ],
    [],
]
AFTER = [
    ("rb", 2), ("ra", 1), ("rx", 3), ("py", 2), ("pz", 1), ("handle", 0, 3), ("final", 0), ("rx", 2),
    ("ra", 0), ("rb", 1), ("gb", 3), ("px", 3), ("pz", 0), ("py", 1), ("rb", 0), ("settle", 18), ("rx", 1), ("gb", 2),
    ("px", 2), ("ga", 3), ("rx", 0), ("gb", 1), ("ga", 2), ("gb", 0), ("settle", 12), ("ga", 1), ("gc", 3), ("py", 0),
    ("gc", 2), ("px", 1), ("inv", 3), ("ga", 0), ("settle", 6), ("ci", 2), ("inv", 2), ("gc", 1), ("ci", 1),
    ("px", 0), ("inv", 1), ("gc", 0), ("ci", 0), ("inv", 0),
]
LOCAL = 64


def kernel(names, f_hbm, m_hbm, x_hbm, diag_hbm, pat_ref, cols_out, inv_out, *refs):
    v = dict(zip(names, refs))
    send_sem, recv_sem, local_sem, sib_send_sem, sib_recv_sem = refs[len(names):]
    row, col = lax.axis_index("row"), lax.axis_index("col")
    x, core = row // 2, row % 2
    y, z = col // 4, col % 4

    def at(x, y, z, core):
        return ((x % 4) * 2 + core, (y % 4) * 4 + z % 4)

    sibling = at(x, y, z, 1 - core)
    x_peer = [at(x + s, y, z, core) for s in range(4)]
    a_me, b_me = y + (z - y) * core, z + (y - z) * core
    a_peer = [at(x, y + s * (1 - core), z + s * core, core) for s in range(4)]
    b_peer = [at(x, y + s * core, z + s * (1 - core), core) for s in range(4)]
    chunk = (x + y + z) % 4
    to = col * 8 + 2 * chunk + core
    place = (to // 16, to % 16)
    stays = to == row * 16 + col
    rows_c, rows_k = (row * 16 + col) // 8, (row * 16 + col) % 8
    owner = at(rows_k // 2 - rows_c // 4 - rows_c % 4 + 8, rows_c // 4, rows_c % 4, rows_k % 2)
    to_z = at(x, y, chunk % 2 * 2 + core, z // 2)
    to_z_stays = (to_z[0] == row) & (to_z[1] == col)
    z_was = 2 * core + (z // 2 + x + y) % 2
    to_z_source = at(x, y, z_was, z % 2)
    y_next = z_was % 2 * 2 + (x + y + z_was) % 4 // 2
    to_y = at(x, y_next, z, core)
    x_next = (col % 8 // 2 - x - 2 * core - col // 8 + 8) % 4
    to_x = at(x_next, y, z, core)

    other = 1 - core
    a_at = [(a_me + s) % 4 for s in range(4)]
    b_at = [(b_me + s) % 4 for s in range(4)]
    own_rows = pl.ds(pl.multiple_of(col * 128, 128), 128)
    away, away_z, y_here, x_here = jnp.logical_not(stays), jnp.logical_not(to_z_stays), y_next == y, x_next == x
    y_away, x_away = jnp.logical_not(y_here), jnp.logical_not(x_here)

    counts = {"remote": 0, "local": 0}
    pending = []

    class Remote:
        def __init__(self, src, dst, device):
            self.what = src, dst, counts["remote"], device
            counts["remote"] += 1

        def copy(self):
            src, dst, i, device = self.what
            return pltpu.make_async_remote_copy(
                src(), dst(), send_sem.at[i], recv_sem.at[i], device_id=device, device_id_type=MESH
            )

        def start(self):
            self.copy().start()

        def wait_recv(self):
            self.copy().wait_recv()

        def wait_send(self):
            self.copy().wait_send()

    class Local:
        def __init__(self, src, dst):
            self.what = src, dst, counts["local"]
            counts["local"] += 1

        def copy(self):
            src, dst, i = self.what
            return pltpu.make_async_copy(src(), dst(), local_sem.at[i])

        def start(self):
            self.copy().start()

        def wait(self):
            self.copy().wait()

    def send(src, dst, device):
        copy = Remote(src, dst, device)
        copy.start()
        pending.append(copy.wait_send)
        return copy

    def part_of(name, *index):
        return lambda: v[name].at[index]

    xs = [x + 2, x + 1, x + 3, x]
    m_copy = [Local(lambda p=p: m_hbm.at[p], part_of("m32", p)) for p in range(PANELS)]
    f_copy = []
    for t in range(4):
        first = pl.multiple_of(((xs[t] + y + z) % 4) * W, W)
        f_copy.append(Local(lambda first=first: f_hbm.at[:, pl.ds(first, W)], part_of("f32", t)))
    x_copy = [Local(lambda j=j, k=k: x_hbm.at[j, k], part_of("x32", AT[j, k])) for j, k in PAIRS]
    diag_copy = Local(lambda: diag_hbm, lambda: v["diag"])
    for copy in [m_copy[3], *f_copy, m_copy[2], *x_copy, m_copy[1], m_copy[0], diag_copy]:
        copy.start()

    barrier = pltpu.get_barrier_semaphore()
    for device in [sibling, *x_peer[1:], *a_peer[1:], *b_peer[1:]]:
        pl.semaphore_signal(barrier, inc=1, device_id=device, device_id_type=MESH)

    @pl.when(jnp.logical_not(stays))
    def _():
        pl.semaphore_signal(barrier, inc=1, device_id=place, device_id_type=MESH)

    @pl.when(jnp.logical_not(to_z_stays))
    def _():
        pl.semaphore_signal(barrier, inc=1, device_id=to_z_source, device_id_type=MESH)

    pattern = pat_ref[...]

    def member(block):
        return jnp.max(jnp.where(pattern == block, 1.0, 0.0), axis=1, keepdims=True)

    inside = [member(row * 8 + b) for b in range(8)]
    inside_summed = member(col * 4 + chunk)

    def prep(p):
        pltpu.make_async_copy(m_hbm.at[p], v["m32"].at[p], local_sem.at[p]).wait()
        for b in range(8):
            keep = inside[b][3:, :]
            for k in range(PANELS - 1):
                keep = jnp.where(p == k, inside[b][k:k + 1, :], keep)
            high, low = split((v["m32"][p, b * W:(b + 1) * W, :] * keep).T)
            v["mh"][:, b * W:(b + 1) * W] = high
            v["ml"][:, b * W:(b + 1) * W] = low

    own_copy = {}

    def enter():
        pl.semaphore_wait(barrier, 10 + jnp.where(stays, 0, 1) + jnp.where(to_z_stays, 0, 1))
        for p in reversed(range(PANELS)):
            own_copy[p] = Remote(lambda p=p: m_hbm.at[p, own_rows], part_of("own", p), owner)

        @pl.when(away)
        def _():
            for copy in own_copy.values():
                copy.start()

        @pl.when(stays)
        def _():
            for p in range(PANELS):
                copy = Local(lambda p=p: m_hbm.at[p, own_rows], part_of("own", p))
                copy.start()
                copy.wait()

    def prep_own(p):
        @pl.when(away)
        def _():
            own_copy[p].wait_recv()
            own_copy[p].wait_send()

        high, low = split((v["own"][p] * inside_summed[p:p + 1, :]).T)
        v["oh"][p], v["ol"][p] = high, low

    def prep_cross():
        for copy in x_copy:
            copy.wait()
        for i in range(len(PAIRS)):
            block = v["x32"][i]
            v["xh"][i], v["xl"][i] = split(block)
            v["xth"][i], v["xtl"][i] = split(block.T)

    def cross(j, k):
        return v["xh"][AT[j, k]], v["xl"][AT[j, k]]

    def cross_t(j, k):
        return v["xth"][AT[j, k]], v["xtl"][AT[j, k]]

    r1_copy, r2_copy, place_copy = {}, {}, {}
    core_copy, a_copy, b_copy, gx_copy, back = {}, {}, {}, {}, {}
    last = []

    def sib_copy(p, t):
        i = (3 - p) * 4 + t
        return pltpu.make_async_remote_copy(
            v["part"].at[p, t, other], v["sib"].at[p, t], sib_send_sem.at[i], sib_recv_sem.at[i],
            device_id=sibling, device_id_type=MESH,
        )

    def tile(step):
        p, t = 3 - step // 4, step % 4

        @pl.when(t == 0)
        def _():
            prep(p)

        @pl.when(step < 4)
        def _():
            pltpu.make_async_copy(v["f32"].at[t], v["f32"].at[t], local_sem.at[PANELS + t]).wait()
            v["fh"][t], v["fl"][t] = split(v["f32"][t])

        d = dot3((v["mh"][...], v["ml"][...]), (v["fh"][t], v["fl"][t]))
        v["part"][p, t, 0] = d[:, :128]
        v["part"][p, t, 1] = d[:, 128:]

        @pl.when(step == 0)
        def _():
            enter()

        sib_copy(p, t).start()

    def handle(p, t):
        sib_copy(p, t).wait_recv()
        chip = v["chip"].at[p, t]
        chip[...] = v["part"][p, t, core] + v["sib"][p, t]
        if t == 0:
            r1_copy[p, 0] = send(part_of("chip", p, 0, pl.ds(0, 128)), part_of("r1", p, 0), x_peer[1])
            r1_copy[p, 1] = send(part_of("chip", p, 0, pl.ds(128, 128)), part_of("r1", p, 1), x_peer[3])
        if t == 1:
            r2_copy[p, 1] = send(part_of("chip", p, 1, pl.ds(128, 128)), part_of("r2", p, 0, pl.ds(128, 128)), x_peer[1])
        if t == 2:
            r2_copy[p, 2] = send(part_of("chip", p, 2, pl.ds(0, 128)), part_of("r2", p, 1, pl.ds(0, 128)), x_peer[3])

    def combine(p):
        r1_copy[p, 0].wait_recv()
        chip = v["chip"].at[p, 1, :128]
        chip[...] += v["r1"][p, 0]
        r2_copy[p, 0] = send(part_of("chip", p, 1, pl.ds(0, 128)), part_of("r2", p, 0, pl.ds(0, 128)), x_peer[1])
        r1_copy[p, 1].wait_recv()
        chip = v["chip"].at[p, 2, 128:]
        chip[...] += v["r1"][p, 1]
        r2_copy[p, 3] = send(part_of("chip", p, 2, pl.ds(128, 128)), part_of("r2", p, 1, pl.ds(128, 128)), x_peer[3])

    def final(p):
        for i in range(4):
            r2_copy[p, i].wait_recv()
        d = (v["chip"][p, 3] + v["r2"][p, 0] + v["r2"][p, 1]).T
        gram(p, p, split(d))
        if p == 0:
            core_copy[p] = send(part_of("g0", other), lambda: v["gs0"], sibling)
        for j in range(p + 1, PANELS):
            d = d + dot3((v["ch"][j], v["cl"][j]), cross(j, p))
        c = -inside_summed[p:p + 1, :] * d
        v["cols"][p] = c
        if p > 0:
            pair = split(c)
            v["ch"][p], v["cl"][p] = pair
            for k in range(p):
                gram(p, k, pair)
            core_copy[p] = send(part_of(f"g{p}", other), lambda: v[f"gs{p}"], sibling)

    def move(src, dst, device, here, away):
        copy, stay = Remote(src, dst, device), Local(src, dst)

        @pl.when(away)
        def _():
            copy.start()

        @pl.when(here)
        def _():
            stay.start()

        def arrive():
            @pl.when(away)
            def _():
                copy.wait_recv()

            @pl.when(here)
            def _():
                stay.wait()

        def sent():
            @pl.when(away)
            def _():
                copy.wait_send()

        last.append(sent)
        return arrive

    def place_z(p):
        place_copy[p] = move(part_of("cols", p), part_of("midz", p), to_z, to_z_stays, away_z)

    def place_y(p):
        place_copy[p]()
        place_copy[p] = move(part_of("midz", p), part_of("midy", p), to_y, y_here, y_away)

    def place_x(p):
        place_copy[p]()
        place_copy[p] = move(part_of("midy", p), lambda: cols_out.at[p], to_x, x_here, x_away)

    def gram(p, k, right):
        value = dot3((v["oh"][k], v["ol"][k]), right)
        v[f"g{p}"][:, :, :, k] = value.reshape(2, 4, 4, 8, W)

    def reduce_a(p):
        core_copy[p].wait_recv()
        g = v[f"g{p}"].at[core]
        g[...] += v[f"gs{p}"][...]
        for s in range(1, 4):
            a_copy[p, s] = send(part_of(f"g{p}", core, a_at[s]), part_of(f"ga{p}", s - 1), a_peer[s])

    def reduce_b(p):
        g = v[f"g{p}"].at[core, a_me]
        for s in range(1, 4):
            a_copy[p, s].wait_recv()
        g[...] += v[f"ga{p}"][0] + v[f"ga{p}"][1] + v[f"ga{p}"][2]
        for s in range(1, 4):
            b_copy[p, s] = send(part_of(f"g{p}", core, a_me, b_at[s]), part_of(f"gb{p}", s - 1), b_peer[s])

    def reduce_x(p):
        for s in range(1, 4):
            b_copy[p, s].wait_recv()
        gb, gx = v[f"gb{p}"], v[f"gx{p}"]
        gx[x] = v[f"g{p}"][core, a_me, b_me] + gb[0] + gb[1] + gb[2]
        for s in range(1, 4):
            gx_copy[p, s] = send(part_of(f"gx{p}", x), part_of(f"gx{p}", x), x_peer[s])

    def gather_b(p):
        for s in range(1, 4):
            gx_copy[p, s].wait_recv()
        gx, res_at = v[f"gx{p}"], part_of(f"res{p}", core, a_me, b_me)
        v[f"res{p}"][core, a_me, b_me] = (gx[0] + gx[1]) + (gx[2] + gx[3])
        for s in range(1, 4):
            back[p, "b", s] = send(res_at, res_at, b_peer[s])

    def gather_a(p):
        for s in range(1, 4):
            back[p, "b", s].wait_recv()
        res_at = part_of(f"res{p}", core, a_me)
        for s in range(1, 4):
            back[p, "a", s] = send(res_at, res_at, a_peer[s])

    def gather_core(p):
        for key, copy in back.items():
            if key[:2] == (p, "a"):
                copy.wait_recv()
        res_at = part_of(f"res{p}", core)
        back[p, "core"] = send(res_at, res_at, sibling)

    def block(p, k):
        return v[f"res{p}"][:, :, :, k].reshape(W, W)

    def cross_inverse(k):
        later = list(range(k + 1, PANELS))
        total = v["diag"][k]
        for j in later:
            running = block(j, k)
            total = total + dot3(split(running), cross(j, k))
            for i in later:
                right = v["invt"][j] if i == j else inv_out[i, j]
                running = running + dot3(cross_t(i, k), split(right))
            inv_out[k, j] = -running
            inv_out[j, k] = -running.T
            total = total + dot3(cross_t(j, k), split(running.T))
        v["pre"][...] = total

    def diagonal(k):
        back[k, "core"].wait_recv()
        value = v["pre"][...] + block(k, k)
        inv_out[k, k] = value
        if k > 0:
            v["invt"][k] = value.T

    def start_diag():
        diag_copy.wait()
        v["pre"][...] = v["diag"][3]

    def settle(keep=0):
        while len(pending) > keep:
            pending.pop(0)()

    steps = {
        "handle": handle, "combine": combine, "own": prep_own, "cross": prep_cross, "diag": start_diag,
        "final": final, "ra": reduce_a, "rb": reduce_b, "rx": reduce_x, "gb": gather_b, "ga": gather_a,
        "gc": gather_core, "inv": diagonal, "ci": cross_inverse, "pz": place_z, "py": place_y, "px": place_x, "settle": settle,
    }

    def take(order):
        for name, *where in order:
            steps[name](*where)

    @pl.loop(0, 16)
    def _(step):
        tile(step)
        for i, order in enumerate(BETWEEN):
            if order:
                pl.when(step == i)(lambda order=order: take(order))

    take(AFTER)
    for p in range(PANELS):
        for t in range(4):
            sib_copy(p, t).wait_send()
    settle()
    for p in range(PANELS):
        place_copy[p]()
    for finish in last:
        finish()


def copy_kernel(cols_in, inv_in, cols_hbm, inv_hbm, sem):
    copies = [
        pltpu.make_async_copy(cols_in, cols_hbm, sem.at[0]),
        *[pltpu.make_async_copy(inv_in.at[k], inv_hbm.at[k], sem.at[1 + k]) for k in range(PANELS)],
    ]
    for copy in copies:
        copy.start()
    for copy in copies:
        copy.wait()


def shards(front_inverse, panel_front, panel_cross, diag_inverse, pattern):
    s = scratch()
    hbm, vmem = pl.BlockSpec(memory_space=pl.ANY), pl.BlockSpec(memory_space=pltpu.VMEM)
    shapes = (PANELS, 128, W), (PANELS, PANELS, W, W)

    def body(*refs):
        kernel(s.names, *refs)

    held = pl.pallas_call(
        body,
        out_shape=tuple(pltpu.VMEM(shape, F32) for shape in shapes),
        in_specs=[hbm] * 4 + [vmem],
        out_specs=(vmem, vmem),
        scratch_shapes=s.shapes + [
            pltpu.SemaphoreType.DMA((REMOTE,)),
            pltpu.SemaphoreType.DMA((REMOTE,)),
            pltpu.SemaphoreType.DMA((LOCAL,)),
            pltpu.SemaphoreType.DMA((16,)),
            pltpu.SemaphoreType.DMA((16,)),
        ],
        compiler_params=pltpu.CompilerParams(
            collective_id=0, has_side_effects=True, vmem_limit_bytes=VMEM_LIMIT
        ),
        cost_estimate=pl.CostEstimate(
            flops=3 * 2 * 2048 * 1024 * 1024, bytes_accessed=22 * 2**20, transcendentals=0
        ),
    )(front_inverse, panel_front, panel_cross, diag_inverse, pattern)
    return pl.pallas_call(
        copy_kernel,
        out_shape=tuple(jax.ShapeDtypeStruct(shape, F32) for shape in shapes),
        in_specs=[vmem, vmem],
        out_specs=(hbm, hbm),
        scratch_shapes=[pltpu.SemaphoreType.DMA((1 + PANELS,))],
        compiler_params=pltpu.CompilerParams(vmem_limit_bytes=8 * 2**20),
    )(*held)


def solution(mesh):
    in_specs = (P("row", "col"), P(None, "row", None), P(), P(), P())
    out_specs = (P(None, ("row", "col"), None), P())
    return jax.shard_map(shards, mesh=mesh, in_specs=in_specs, out_specs=out_specs, check_vma=False)
```

```python
import jax
import jax.numpy as jnp
from jax import lax
from jax.experimental import pallas as pl
from jax.experimental.pallas import tpu as pltpu
from jax.sharding import PartitionSpec as P

MESH = pl.DeviceIdType.MESH
F32, BF16 = jnp.float32, jnp.bfloat16
W = 256
PANELS = 4
PAIRS = [(j, k) for k in range(PANELS) for j in range(k + 1, PANELS)]
AT = {pair: i for i, pair in enumerate(PAIRS)}


def split(value):
    high = value.astype(BF16)
    return high, (value - high.astype(F32)).astype(BF16)


def dot(left, right):
    return jnp.dot(left, right, preferred_element_type=F32)


def dot3(left, right):
    return dot(left[0], right[0]) + dot(left[1], right[0]) + dot(left[0], right[1])


class Scratch:
    def __init__(self):
        self.names, self.shapes = [], []

    def add(self, name, shape, dtype=F32):
        self.names.append(name)
        self.shapes.append(pltpu.VMEM(shape, dtype))


def scratch():
    s = Scratch()
    s.add("m32", (PANELS, 2048, W))
    s.add("f32", (4, 2048, W))
    s.add("fh", (4, 2048, W), BF16)
    s.add("fl", (4, 2048, W), BF16)
    s.add("mh", (W, 2048), BF16)
    s.add("ml", (W, 2048), BF16)
    s.add("part", (PANELS, 4, 2, W, 128))
    s.add("sib", (PANELS, 4, W, 128))
    s.add("chip", (PANELS, 4, W, 128))
    s.add("r1", (PANELS, 2, 128, 128))
    s.add("r2", (PANELS, 2, W, 128))
    s.add("cols", (PANELS, 128, W))
    s.add("ch", (PANELS, 128, W), BF16)
    s.add("cl", (PANELS, 128, W), BF16)
    s.add("own", (PANELS, 128, W))
    s.add("midz", (PANELS, 128, W))
    s.add("midy", (PANELS, 128, W))
    s.add("oh", (PANELS, W, 128), BF16)
    s.add("ol", (PANELS, W, 128), BF16)
    s.add("x32", (len(PAIRS), W, W))
    for name in ("xh", "xl", "xth", "xtl"):
        s.add(name, (len(PAIRS), W, W), BF16)
    s.add("diag", (PANELS, W, W))
    for p in range(PANELS):
        n = p + 1
        s.add(f"g{p}", (2, 4, 4, n, 8, W))
        s.add(f"gs{p}", (4, 4, n, 8, W))
        s.add(f"ga{p}", (3, 4, n, 8, W))
        s.add(f"gb{p}", (3, n, 8, W))
        s.add(f"gx{p}", (4, n, 8, W))
        s.add(f"res{p}", (2, 4, 4, n, 8, W))
    s.add("invt", (PANELS, W, W))
    s.add("pre", (W, W))
    return s


REMOTE = 192
VMEM_LIMIT = 58 * 2**20
BETWEEN = [
    [],
    [],
    [
        ("handle", 3, 0),
    ],
    [],
    [
        ("handle", 3, 3),
    ],
    [
        ("handle", 3, 2), ("handle", 3, 1),
    ],
    [],
    [
        ("handle", 2, 0),
    ],
    [
        ("own", 3), ("combine", 3), ("cross",), ("diag",), ("handle", 1, 0), ("handle", 2, 3),
    ],
    [
        ("handle", 2, 1), ("handle", 2, 2), ("own", 2), ("combine", 2), ("handle", 1, 1),
    ],
    [
        ("own", 1), ("own", 0), ("final", 3), ("pz", 3),
    ],
    [
        ("handle", 1, 2), ("combine", 1), ("ra", 3),
    ],
    [
        ("final", 2), ("pz", 2), ("handle", 0, 0),
    ],
    [
        ("ra", 2),
    ],
    [
        ("rb", 3), ("handle", 0, 1), ("handle", 1, 3), ("py", 3), ("handle", 0, 2), ("combine", 0),
        ("final", 1),
    ],
    [],
]
AFTER = [
    ("rb", 2), ("ra", 1), ("rx", 3), ("py", 2), ("pz", 1), ("handle", 0, 3), ("final", 0), ("rx", 2),
    ("ra", 0), ("rb", 1), ("gb", 3), ("px", 3), ("pz", 0), ("py", 1), ("rb", 0), ("settle", 18), ("rx", 1),
    ("gb", 2), ("px", 2), ("ga", 3), ("rx", 0), ("py", 0), ("gb", 1), ("ga", 2), ("gb", 0), ("settle", 12),
    ("ga", 1), ("gc", 3), ("px", 1), ("gc", 2), ("px", 0), ("ga", 0), ("settle", 6), ("inv", 3), ("ci", 2),
    ("inv", 2), ("gc", 1), ("ci", 1), ("inv", 1), ("gc", 0), ("ci", 0), ("inv", 0),
]
LOCAL = 64


def kernel(names, f_hbm, m_hbm, x_hbm, diag_hbm, pat_ref, cols_out, inv_out, *refs):
    v = dict(zip(names, refs))
    send_sem, recv_sem, local_sem, sib_send_sem, sib_recv_sem = refs[len(names):]
    row, col = lax.axis_index("row"), lax.axis_index("col")
    x, core = row // 2, row % 2
    y, z = col // 4, col % 4

    def at(x, y, z, core):
        return ((x % 4) * 2 + core, (y % 4) * 4 + z % 4)

    sibling = at(x, y, z, 1 - core)
    x_peer = [at(x + s, y, z, core) for s in range(4)]
    a_me, b_me = y + (z - y) * core, z + (y - z) * core
    a_peer = [at(x, y + s * (1 - core), z + s * core, core) for s in range(4)]
    b_peer = [at(x, y + s * core, z + s * (1 - core), core) for s in range(4)]
    chunk = (x + y + z) % 4
    to = col * 8 + 2 * chunk + core
    place = (to // 16, to % 16)
    stays = to == row * 16 + col
    rows_c, rows_k = (row * 16 + col) // 8, (row * 16 + col) % 8
    owner = at(rows_k // 2 - rows_c // 4 - rows_c % 4 + 8, rows_c // 4, rows_c % 4, rows_k % 2)
    to_z = at(x, y, chunk % 2 * 2 + core, z // 2)
    to_z_stays = (to_z[0] == row) & (to_z[1] == col)
    z_was = 2 * core + (z // 2 + x + y) % 2
    to_z_source = at(x, y, z_was, z % 2)
    y_next = z_was % 2 * 2 + (x + y + z_was) % 4 // 2
    to_y = at(x, y_next, z, core)
    x_next = (col % 8 // 2 - x - 2 * core - col // 8 + 8) % 4
    to_x = at(x_next, y, z, core)

    other = 1 - core
    a_at = [(a_me + s) % 4 for s in range(4)]
    b_at = [(b_me + s) % 4 for s in range(4)]
    own_rows = pl.ds(pl.multiple_of(col * 128, 128), 128)
    away, away_z, y_here, x_here = jnp.logical_not(stays), jnp.logical_not(to_z_stays), y_next == y, x_next == x
    y_away, x_away = jnp.logical_not(y_here), jnp.logical_not(x_here)

    counts = {"remote": 0, "local": 0}
    pending = []

    class Remote:
        def __init__(self, src, dst, device):
            self.what = src, dst, counts["remote"], device
            counts["remote"] += 1

        def copy(self):
            src, dst, i, device = self.what
            return pltpu.make_async_remote_copy(
                src(), dst(), send_sem.at[i], recv_sem.at[i], device_id=device, device_id_type=MESH
            )

        def start(self):
            self.copy().start()

        def wait_recv(self):
            self.copy().wait_recv()

        def wait_send(self):
            self.copy().wait_send()

    class Local:
        def __init__(self, src, dst):
            self.what = src, dst, counts["local"]
            counts["local"] += 1

        def copy(self):
            src, dst, i = self.what
            return pltpu.make_async_copy(src(), dst(), local_sem.at[i])

        def start(self):
            self.copy().start()

        def wait(self):
            self.copy().wait()

    def send(src, dst, device):
        copy = Remote(src, dst, device)
        copy.start()
        pending.append(copy.wait_send)
        return copy

    def part_of(name, *index):
        return lambda: v[name].at[index]

    xs = [x + 2, x + 1, x + 3, x]
    m_copy = [Local(lambda p=p: m_hbm.at[p], part_of("m32", p)) for p in range(PANELS)]
    f_copy = []
    for t in range(4):
        first = pl.multiple_of(((xs[t] + y + z) % 4) * W, W)
        f_copy.append(Local(lambda first=first: f_hbm.at[:, pl.ds(first, W)], part_of("f32", t)))
    x_copy = [Local(lambda j=j, k=k: x_hbm.at[j, k], part_of("x32", AT[j, k])) for j, k in PAIRS]
    diag_copy = Local(lambda: diag_hbm, lambda: v["diag"])
    for copy in [m_copy[3], *f_copy, m_copy[2], *x_copy, m_copy[1], m_copy[0], diag_copy]:
        copy.start()

    barrier = pltpu.get_barrier_semaphore()
    for device in [sibling, *x_peer[1:], *a_peer[1:], *b_peer[1:]]:
        pl.semaphore_signal(barrier, inc=1, device_id=device, device_id_type=MESH)

    @pl.when(jnp.logical_not(stays))
    def _():
        pl.semaphore_signal(barrier, inc=1, device_id=place, device_id_type=MESH)

    @pl.when(jnp.logical_not(to_z_stays))
    def _():
        pl.semaphore_signal(barrier, inc=1, device_id=to_z_source, device_id_type=MESH)

    pattern = pat_ref[...]

    def member(block):
        return jnp.max(jnp.where(pattern == block, 1.0, 0.0), axis=1, keepdims=True)

    inside = [member(row * 8 + b) for b in range(8)]
    inside_summed = member(col * 4 + chunk)

    def prep(p):
        pltpu.make_async_copy(m_hbm.at[p], v["m32"].at[p], local_sem.at[p]).wait()
        for b in range(8):
            keep = inside[b][3:, :]
            for k in range(PANELS - 1):
                keep = jnp.where(p == k, inside[b][k:k + 1, :], keep)
            high, low = split((v["m32"][p, b * W:(b + 1) * W, :] * keep).T)
            v["mh"][:, b * W:(b + 1) * W] = high
            v["ml"][:, b * W:(b + 1) * W] = low

    own_copy = {}

    def enter():
        pl.semaphore_wait(barrier, 10 + jnp.where(stays, 0, 1) + jnp.where(to_z_stays, 0, 1))
        for p in reversed(range(PANELS)):
            own_copy[p] = Remote(lambda p=p: m_hbm.at[p, own_rows], part_of("own", p), owner)

        @pl.when(away)
        def _():
            for copy in own_copy.values():
                copy.start()

        @pl.when(stays)
        def _():
            for p in range(PANELS):
                copy = Local(lambda p=p: m_hbm.at[p, own_rows], part_of("own", p))
                copy.start()
                copy.wait()

    def prep_own(p):
        @pl.when(away)
        def _():
            own_copy[p].wait_recv()
            own_copy[p].wait_send()

        high, low = split((v["own"][p] * inside_summed[p:p + 1, :]).T)
        v["oh"][p], v["ol"][p] = high, low

    def prep_cross():
        for copy in x_copy:
            copy.wait()
        for i in range(len(PAIRS)):
            block = v["x32"][i]
            v["xh"][i], v["xl"][i] = split(block)
            v["xth"][i], v["xtl"][i] = split(block.T)

    def cross(j, k):
        return v["xh"][AT[j, k]], v["xl"][AT[j, k]]

    def cross_t(j, k):
        return v["xth"][AT[j, k]], v["xtl"][AT[j, k]]

    r1_copy, r2_copy, place_copy = {}, {}, {}
    core_copy, a_copy, b_copy, gx_copy, back = {}, {}, {}, {}, {}
    last = []

    def sib_copy(p, t):
        i = (3 - p) * 4 + t
        return pltpu.make_async_remote_copy(
            v["part"].at[p, t, other], v["sib"].at[p, t], sib_send_sem.at[i], sib_recv_sem.at[i],
            device_id=sibling, device_id_type=MESH,
        )

    def tile(step):
        p, t = 3 - step // 4, step % 4

        @pl.when(t == 0)
        def _():
            prep(p)

        @pl.when(step < 4)
        def _():
            pltpu.make_async_copy(v["f32"].at[t], v["f32"].at[t], local_sem.at[PANELS + t]).wait()
            v["fh"][t], v["fl"][t] = split(v["f32"][t])

        d = dot3((v["mh"][...], v["ml"][...]), (v["fh"][t], v["fl"][t]))
        v["part"][p, t, 0] = d[:, :128]
        v["part"][p, t, 1] = d[:, 128:]

        @pl.when(step == 0)
        def _():
            enter()

        sib_copy(p, t).start()

    def handle(p, t):
        sib_copy(p, t).wait_recv()
        chip = v["chip"].at[p, t]
        chip[...] = v["part"][p, t, core] + v["sib"][p, t]
        if t == 0:
            r1_copy[p, 0] = send(part_of("chip", p, 0, pl.ds(0, 128)), part_of("r1", p, 0), x_peer[1])
            r1_copy[p, 1] = send(part_of("chip", p, 0, pl.ds(128, 128)), part_of("r1", p, 1), x_peer[3])
        if t == 1:
            r2_copy[p, 1] = send(part_of("chip", p, 1, pl.ds(128, 128)), part_of("r2", p, 0, pl.ds(128, 128)), x_peer[1])
        if t == 2:
            r2_copy[p, 2] = send(part_of("chip", p, 2, pl.ds(0, 128)), part_of("r2", p, 1, pl.ds(0, 128)), x_peer[3])

    def combine(p):
        r1_copy[p, 0].wait_recv()
        chip = v["chip"].at[p, 1, :128]
        chip[...] += v["r1"][p, 0]
        r2_copy[p, 0] = send(part_of("chip", p, 1, pl.ds(0, 128)), part_of("r2", p, 0, pl.ds(0, 128)), x_peer[1])
        r1_copy[p, 1].wait_recv()
        chip = v["chip"].at[p, 2, 128:]
        chip[...] += v["r1"][p, 1]
        r2_copy[p, 3] = send(part_of("chip", p, 2, pl.ds(128, 128)), part_of("r2", p, 1, pl.ds(128, 128)), x_peer[3])

    def final(p):
        for i in range(4):
            r2_copy[p, i].wait_recv()
        d = (v["chip"][p, 3] + v["r2"][p, 0] + v["r2"][p, 1]).T
        gram(p, p, split(d))
        if p == 0:
            core_copy[p] = send(part_of("g0", other), lambda: v["gs0"], sibling)
        for j in range(p + 1, PANELS):
            d = d + dot3((v["ch"][j], v["cl"][j]), cross(j, p))
        c = -inside_summed[p:p + 1, :] * d
        v["cols"][p] = c
        if p > 0:
            pair = split(c)
            v["ch"][p], v["cl"][p] = pair
            for k in range(p):
                gram(p, k, pair)
            core_copy[p] = send(part_of(f"g{p}", other), lambda: v[f"gs{p}"], sibling)

    def move(src, dst, device, here, away):
        copy, stay = Remote(src, dst, device), Local(src, dst)

        @pl.when(away)
        def _():
            copy.start()

        @pl.when(here)
        def _():
            stay.start()

        def arrive():
            @pl.when(away)
            def _():
                copy.wait_recv()

            @pl.when(here)
            def _():
                stay.wait()

        def sent():
            @pl.when(away)
            def _():
                copy.wait_send()

        last.append(sent)
        return arrive

    def place_z(p):
        place_copy[p] = move(part_of("cols", p), part_of("midz", p), to_z, to_z_stays, away_z)

    def place_y(p):
        place_copy[p]()
        place_copy[p] = move(part_of("midz", p), part_of("midy", p), to_y, y_here, y_away)

    def place_x(p):
        place_copy[p]()
        place_copy[p] = move(part_of("midy", p), lambda: cols_out.at[p], to_x, x_here, x_away)

    def gram(p, k, right):
        value = dot3((v["oh"][k], v["ol"][k]), right)
        v[f"g{p}"][:, :, :, k] = value.reshape(2, 4, 4, 8, W)

    def reduce_a(p):
        core_copy[p].wait_recv()
        g = v[f"g{p}"].at[core]
        g[...] += v[f"gs{p}"][...]
        for s in range(1, 4):
            a_copy[p, s] = send(part_of(f"g{p}", core, a_at[s]), part_of(f"ga{p}", s - 1), a_peer[s])

    def reduce_b(p):
        g = v[f"g{p}"].at[core, a_me]
        for s in range(1, 4):
            a_copy[p, s].wait_recv()
        g[...] += v[f"ga{p}"][0] + v[f"ga{p}"][1] + v[f"ga{p}"][2]
        for s in range(1, 4):
            b_copy[p, s] = send(part_of(f"g{p}", core, a_me, b_at[s]), part_of(f"gb{p}", s - 1), b_peer[s])

    def reduce_x(p):
        for s in range(1, 4):
            b_copy[p, s].wait_recv()
        gb, gx = v[f"gb{p}"], v[f"gx{p}"]
        gx[x] = v[f"g{p}"][core, a_me, b_me] + gb[0] + gb[1] + gb[2]
        for s in range(1, 4):
            gx_copy[p, s] = send(part_of(f"gx{p}", x), part_of(f"gx{p}", x), x_peer[s])

    def gather_b(p):
        for s in range(1, 4):
            gx_copy[p, s].wait_recv()
        gx, res_at = v[f"gx{p}"], part_of(f"res{p}", core, a_me, b_me)
        v[f"res{p}"][core, a_me, b_me] = (gx[0] + gx[1]) + (gx[2] + gx[3])
        for s in range(1, 4):
            back[p, "b", s] = send(res_at, res_at, b_peer[s])

    def gather_a(p):
        for s in range(1, 4):
            back[p, "b", s].wait_recv()
        res_at = part_of(f"res{p}", core, a_me)
        for s in range(1, 4):
            back[p, "a", s] = send(res_at, res_at, a_peer[s])

    def gather_core(p):
        for key, copy in back.items():
            if key[:2] == (p, "a"):
                copy.wait_recv()
        res_at = part_of(f"res{p}", core)
        back[p, "core"] = send(res_at, res_at, sibling)

    def block(p, k):
        return v[f"res{p}"][:, :, :, k].reshape(W, W)

    def cross_inverse(k):
        later = list(range(k + 1, PANELS))
        total = v["diag"][k]
        for j in later:
            running = block(j, k)
            total = total + dot3(split(running), cross(j, k))
            for i in later:
                right = v["invt"][j] if i == j else inv_out[i, j]
                running = running + dot3(cross_t(i, k), split(right))
            inv_out[k, j] = -running
            inv_out[j, k] = -running.T
            total = total + dot3(cross_t(j, k), split(running.T))
        v["pre"][...] = total

    def diagonal(k):
        back[k, "core"].wait_recv()
        value = v["pre"][...] + block(k, k)
        inv_out[k, k] = value
        if k > 0:
            v["invt"][k] = value.T

    def start_diag():
        diag_copy.wait()
        v["pre"][...] = v["diag"][3]

    def settle(keep=0):
        while len(pending) > keep:
            pending.pop(0)()

    steps = {
        "handle": handle, "combine": combine, "own": prep_own, "cross": prep_cross, "diag": start_diag,
        "final": final, "ra": reduce_a, "rb": reduce_b, "rx": reduce_x, "gb": gather_b, "ga": gather_a,
        "gc": gather_core, "inv": diagonal, "ci": cross_inverse, "pz": place_z, "py": place_y, "px": place_x, "settle": settle,
    }

    def take(order):
        for name, *where in order:
            steps[name](*where)

    @pl.loop(0, 16)
    def _(step):
        tile(step)
        for i, order in enumerate(BETWEEN):
            if order:
                pl.when(step == i)(lambda order=order: take(order))

    take(AFTER)
    for p in range(PANELS):
        for t in range(4):
            sib_copy(p, t).wait_send()
    settle()
    for p in range(PANELS):
        place_copy[p]()
    for finish in last:
        finish()


def copy_kernel(cols_in, inv_in, cols_hbm, inv_hbm, sem):
    copies = [
        pltpu.make_async_copy(cols_in, cols_hbm, sem.at[0]),
        *[pltpu.make_async_copy(inv_in.at[k], inv_hbm.at[k], sem.at[1 + k]) for k in range(PANELS)],
    ]
    for copy in copies:
        copy.start()
    for copy in copies:
        copy.wait()


def shards(front_inverse, panel_front, panel_cross, diag_inverse, pattern):
    s = scratch()
    hbm, vmem = pl.BlockSpec(memory_space=pl.ANY), pl.BlockSpec(memory_space=pltpu.VMEM)
    shapes = (PANELS, 128, W), (PANELS, PANELS, W, W)

    def body(*refs):
        kernel(s.names, *refs)

    held = pl.pallas_call(
        body,
        out_shape=tuple(pltpu.VMEM(shape, F32) for shape in shapes),
        in_specs=[hbm] * 4 + [vmem],
        out_specs=(vmem, vmem),
        scratch_shapes=s.shapes + [
            pltpu.SemaphoreType.DMA((REMOTE,)),
            pltpu.SemaphoreType.DMA((REMOTE,)),
            pltpu.SemaphoreType.DMA((LOCAL,)),
            pltpu.SemaphoreType.DMA((16,)),
            pltpu.SemaphoreType.DMA((16,)),
        ],
        compiler_params=pltpu.CompilerParams(
            collective_id=0, has_side_effects=True, vmem_limit_bytes=VMEM_LIMIT
        ),
        cost_estimate=pl.CostEstimate(
            flops=3 * 2 * 2048 * 1024 * 1024, bytes_accessed=22 * 2**20, transcendentals=0
        ),
    )(front_inverse, panel_front, panel_cross, diag_inverse, pattern)
    return pl.pallas_call(
        copy_kernel,
        out_shape=tuple(jax.ShapeDtypeStruct(shape, F32) for shape in shapes),
        in_specs=[vmem, vmem],
        out_specs=(hbm, hbm),
        scratch_shapes=[pltpu.SemaphoreType.DMA((1 + PANELS,))],
        compiler_params=pltpu.CompilerParams(vmem_limit_bytes=8 * 2**20),
    )(*held)


def solution(mesh):
    in_specs = (P("row", "col"), P(None, "row", None), P(), P(), P())
    out_specs = (P(None, ("row", "col"), None), P())
    return jax.shard_map(shards, mesh=mesh, in_specs=in_specs, out_specs=out_specs, check_vma=False)
```
